256 devices in a mesh: heads: 8 (over y, x_lo), ctx: 32 (over z, x_hi, core).
Axes of the slice: x: 4 (x_hi: 2, x_lo: 2; x = x_hi * 2 + x_lo), y: 4, z: 8, core: 2. Of those that a mesh axis runs over, the one named last changes fastest.
Arguments:
- query: float32 [4096, 8192], P('ctx', 'heads'), parts along dimension 1, may hold values from -6 to 6
- key: float32 [4096, 1024], P('ctx', 'heads'), parts along dimension 1, may hold values from -6 to 6
- value: float32 [4096, 1024], P('ctx', 'heads'), parts along dimension 1, may hold values from -6 to 6
- output: float32 [4096, 8192], P('ctx', 'heads'), parts along dimension 1, may hold values from -6 to 6
- grad_output: float32 [4096, 8192], P('ctx', 'heads'), parts along dimension 1, may hold values from -6 to 6
- lse: float32 [64, 4096], P('heads', 'ctx'), parts along dimension 0, may hold values from -0.5 to 20, as said below
- span_order: int32 [512], P('heads'), parts along dimension 0, may hold values from 0 to 63, as said below
Outputs:
- grad_query: float32 [4096, 8192], P('ctx', 'heads'), parts along dimension 1
- grad_key: float32 [4096, 1024], P('ctx', 'heads'), parts along dimension 1
- grad_value: float32 [4096, 1024], P('ctx', 'heads'), parts along dimension 1
The draws below stay inside these ranges and needn't reach their ends.
There are 8 independent parts, one for each index of `heads`. The reference program is written for one: setup_inputs(seed, part) draws one part's arguments, and reference() takes and returns one part's arrays. A program takes and returns all parts, laid end to end along the dimension named above; each array names one. Nothing has to cross between parts.
Inputs may be any that keep to these rules, and one draw needn't show every extreme that they name: `span_order`: a permutation: each of 0 to 63 once. `lse`: log of the row's causal key count, plus 0.5, plus a perturbation.
All inputs are finite; a program needn't handle non-finite values.
Results may differ from the reference program's by a relative error of at most 0.0003.
Values sent between devices are 32-bit elements; how exact they have to be, the bound alone decides.
No kernel may reach another device: no remote copies, remote signals or barrier semaphores. Data moves between devices by JAX's collectives and lax.ppermute only.
A program may use at most 64 MiB of HBM per device.

```python
import math
import jax
import jax.numpy as jnp
from jax import lax

DH = 128
HQ = 8
TOK_DEV = 128
SEQ = 4096
SPANS = 64


def shared_order(key):
    return jax.random.permutation(key, SPANS).astype(jnp.int32)


def draw_span_order(key, part):
    return shared_order(key)


def draw_lse(key, part):
    order = shared_order(key)
    key = jax.random.fold_in(key, 7)
    half = TOK_DEV // 2
    rows = jnp.arange(SEQ, dtype=jnp.int32)
    pos = order[rows // half] * half + rows % half
    base = jnp.log(pos.astype(jnp.float32) + 1.0) + 0.5
    noise = 0.2 * jnp.clip(jax.random.normal(key, (HQ, SEQ), jnp.float32), -2.0, 2.0)
    return (base[None, :] + noise).astype(jnp.float32)


def block_levels(stream_key, dims, cuts, smallest, top_value):
    level = 1.0
    for axis_at, parts in cuts:
        steps = jax.random.uniform(jax.random.fold_in(jax.random.fold_in(stream_key, 6), axis_at), (parts,), jnp.float32, smallest / len(cuts), top_value / len(cuts))
        level = level * jnp.repeat(jnp.exp(steps), dims[axis_at] // parts).reshape((-1,) + (1,) * (len(dims) - 1 - axis_at))
    return level


def scatter_about(key, extent, spread, most, shards=(), held_as=jnp.bfloat16):
    level = block_levels(key, extent, shards, -0.22, 0.18) if shards else 1.0
    entries = jax.random.normal(key, extent, jnp.float32) * spread * level
    return jnp.minimum(jnp.maximum(entries, -most), most).astype(held_as)


def setup_inputs(seed: int = 0, part: int = 0) -> dict:
    seeds = jax.random.split(jax.random.key(seed), 8)
    part_keys = jax.random.split(jax.random.fold_in(seeds[7], part), 8)
    query = scatter_about(part_keys[0], (SEQ, HQ * DH), 1.0, 6.0, ((0, 32),), jnp.float32)
    key = scatter_about(part_keys[1], (SEQ, DH), 1.0, 6.0, ((0, 32),), jnp.float32)
    value = scatter_about(part_keys[2], (SEQ, DH), 1.0, 6.0, ((0, 32),), jnp.float32)
    output = scatter_about(part_keys[3], (SEQ, HQ * DH), 1.0, 6.0, ((0, 32),), jnp.float32)
    grad_output = scatter_about(part_keys[4], (SEQ, HQ * DH), 1.0, 6.0, ((0, 32),), jnp.float32)
    lse = draw_lse(jax.random.fold_in(jax.random.fold_in(seeds[7], part), 71), part)
    span_order = draw_span_order(jax.random.fold_in(jax.random.fold_in(seeds[7], part), 71), part)
    return {"query": query, "key": key, "value": value, "output": output, "grad_output": grad_output, "lse": lse, "span_order": span_order}


def positions(order, first, count, half):
    rows = first + jnp.arange(count, dtype=jnp.int32)
    slots = rows // half
    hits = slots[:, None] == jnp.arange(order.shape[0], dtype=jnp.int32)[None, :]
    base = lax.optimization_barrier(jnp.sum(jnp.where(hits, order[None, :], 0), axis=1)).astype(jnp.int32)
    return base * half + rows % half

def tile_grads(qheads, dout, lse_rows, delta, qpos, kblock, vblock, kpos, scale):
    highest = lax.Precision.HIGHEST
    scores = jnp.einsum('qhd,kd->hqk', qheads, kblock, precision=highest) * scale
    visible = kpos[None, :] <= qpos[:, None]
    prob = jnp.exp(jnp.where(visible[None], scores - lse_rows[:, :, None], -1e+30))
    dprob = jnp.einsum('qhd,kd->hqk', dout, vblock, precision=highest)
    dscore = prob * (dprob - delta[:, :, None])
    grad_q = jnp.einsum('hqk,kd->qhd', dscore, kblock, precision=highest) * scale
    grad_k = jnp.einsum('hqk,qhd->kd', dscore, qheads, precision=highest) * scale
    grad_v = jnp.einsum('hqk,qhd->kd', prob, dout, precision=highest)
    return (grad_q, grad_k, grad_v)

def reference(query, key, value, output, grad_output, lse, span_order):
    seq = key.shape[0]
    half = TOK_DEV // 2
    scale = 1.0 / math.sqrt(DH)
    pos = positions(span_order, 0, seq, half)
    qheads = query.reshape(seq, HQ, DH)
    dout = grad_output.reshape(seq, HQ, DH)
    oheads = output.reshape(seq, HQ, DH)
    delta = lax.optimization_barrier(jnp.sum(dout * oheads, axis=2)).T
    blocks = seq // TOK_DEV

    def step(carry, index):
        acc_k, acc_v = carry
        first = (index * TOK_DEV).astype(jnp.int32)
        qblock = lax.dynamic_slice_in_dim(qheads, first, TOK_DEV, 0)
        dblock = lax.dynamic_slice_in_dim(dout, first, TOK_DEV, 0)
        lblock = lax.dynamic_slice_in_dim(lse, first, TOK_DEV, 1)
        eblock = lax.dynamic_slice_in_dim(delta, first, TOK_DEV, 1)
        pblock = lax.dynamic_slice_in_dim(pos, first, TOK_DEV, 0)
        grad_q, grad_k, grad_v = tile_grads(qblock, dblock, lblock, eblock, pblock, key, value, pos, scale)
        return ((acc_k + grad_k, acc_v + grad_v), grad_q)
    zeros = jnp.zeros((seq, DH), jnp.float32)
    (grad_key, grad_value), grad_blocks = lax.scan(step, (zeros, zeros), jnp.arange(blocks, dtype=jnp.int32))
    return (grad_blocks.reshape(seq, HQ * DH), grad_key, grad_value)
```

```python
import functools
import math

import jax
import jax.numpy as jnp
from jax import lax
from jax.experimental import pallas as pl
from jax.experimental.pallas import tpu as pltpu
from jax.sharding import PartitionSpec as P

ZS = 8
DH = 128
HQ = 8
LOG2E = 1.4426950408889634
BIG = 1e30
F32 = jnp.float32
BF16 = jnp.bfloat16
NT = (((1,), (1,)), ((), ()))
NN = (((1,), (0,)), ((), ()))
TN = (((0,), (0,)), ((), ()))


def send(x, dz=0, dx=0, dc=0):
    perm = []
    for z in range(ZS):
        for xh in range(2):
            for c in range(2):
                to = ((z + dz) % ZS) * 4 + ((xh + dx) % 2) * 2 + (c + dc) % 2
                perm.append((z * 4 + xh * 2 + c, to))
    return lax.ppermute(x, "ctx", perm)


def split(x):
    hi = x.astype(BF16)
    return hi, (x - hi.astype(F32)).astype(BF16)


def dot(a, b, dims=NN):
    return lax.dot_general(a, b, dims, preferred_element_type=F32)


def pack_kernel(q_ref, do_ref, o_ref, lse_ref, out_ref):
    out_ref[:, : HQ * DH] = q_ref[...]
    out_ref[:, HQ * DH : 2 * HQ * DH] = do_ref[...]
    rows = q_ref.shape[0]
    lane = lax.broadcasted_iota(jnp.int32, (rows, DH), 1)
    pad = jnp.zeros((DH - HQ, rows), F32)
    extra = jnp.concatenate([lse_ref[...] * (-LOG2E), pad], axis=0).T
    for h in range(HQ):
        s = slice(h * DH, (h + 1) * DH)
        delta = jnp.sum(do_ref[:, s] * o_ref[:, s], axis=1, keepdims=True)
        extra = jnp.where(lane == HQ + h, -delta, extra)
    out_ref[:, 2 * HQ * DH :] = extra


def grads_kernel(offsets, groups, diag, n_kv, has_dq, has_dkv, *refs):
    rank_ref, order_ref, *refs = refs
    nq, nk = len(groups), len(offsets)
    q_refs, do_refs, x_refs = refs[:nq], refs[nq : 2 * nq], refs[2 * nq : 3 * nq]
    refs = refs[3 * nq :]
    kv_refs, refs = refs[:n_kv], refs[n_kv:]
    dq_in, refs = (refs[:nq], refs[nq:]) if has_dq else (None, refs)
    dkv_in, refs = (refs[:nk], refs[nk:]) if has_dkv else (None, refs)
    dq_out, dkv_out, refs = refs[:nq], refs[nq : nq + nk], refs[nq + nk :]
    kc, vc, qc, dc = refs
    h = pl.program_id(0)
    half = DH // 2
    rank = rank_ref[0]
    z, line = rank // 4, rank % 4
    lane = lax.broadcasted_iota(jnp.int32, (half, DH), 1)

    @pl.when(h == 0)
    def _():
        halves = []
        for ref in kv_refs:
            for i in range(ref.shape[0] // half):
                halves.append((ref, i * half))
        for i, (ref, first) in enumerate(halves):
            owner = lax.rem(z + (offsets[i // 2] + ZS), ZS) * 4 + line
            pos = order_ref[owner * 2 + i % 2]
            hot = jnp.where((lane == pos) | ((lane >= 64) & (lane < 67)), 1.0, 0.0).astype(BF16)
            to = slice(i * half, (i + 1) * half)
            hi, lo = split(ref[first : first + half, :DH])
            kc[to, :] = jnp.concatenate([hi, lo, hi, hot], axis=1)
            hi, lo = split(ref[first : first + half, DH:])
            vc[to, :] = jnp.concatenate([hi, lo, hi, hot], axis=1)
        for i in range(nk):
            if has_dkv:
                dkv_out[i][...] = dkv_in[i][...]
            else:
                dkv_out[i][...] = jnp.zeros_like(dkv_out[i])

    for g, (dx, dcore) in enumerate(groups):
        peer = z * 4 + lax.bitwise_xor(line, dx * 2 + dcore)
        for j in range(2):
            s = slice(j * half, (j + 1) * half)
            to = slice(g * DH + j * half, g * DH + (j + 1) * half)
            x = x_refs[g][s, :]
            pos = order_ref[peer * 2 + j]

            def terms(column):
                c = jnp.sum(jnp.where(lane == column, x, 0.0), axis=1, keepdims=True)
                a = c.astype(BF16).astype(F32)
                b = (c - a).astype(BF16).astype(F32)
                d = c - a - b
                return jnp.where(lane == 64, a, jnp.where(lane == 65, b, jnp.where(lane == 66, d, 0.0)))

            bias = jnp.where((lane < 64) & (lane > pos), -BIG, terms(h)).astype(BF16)
            hi, lo = split(q_refs[g][s, :] * (LOG2E / math.sqrt(DH)))
            qc[to, :] = jnp.concatenate([hi, hi, lo, bias], axis=1)
            bias = terms(h + HQ).astype(BF16)
            hi, lo = split(do_refs[g][s, :])
            dc[to, :] = jnp.concatenate([hi, hi, lo, bias], axis=1)

    p = jnp.exp2(dot(kc[...], qc[...], NT))
    if diag:
        a = lax.broadcasted_iota(jnp.int32, p.shape, 0)
        b = lax.broadcasted_iota(jnp.int32, p.shape, 1)
        later = (a < DH) & (b < DH) & (a // half == b // half) & (a > b)
        p = jnp.where(later, 0.0, p)
    ds = p * dot(vc[...], dc[...], NT)
    p_hi, p_lo = split(p)
    r = dot(p_hi, dc[:, DH : 3 * DH])
    dv = r[:, :DH] + r[:, DH:] + dot(p_lo, dc[:, :DH])
    ds_hi, ds_lo = split(ds)
    r = dot(ds_hi, qc[:, DH : 3 * DH])
    dk = (r[:, :DH] + r[:, DH:] + dot(ds_lo, qc[:, :DH])) * (1.0 / LOG2E)
    for i in range(nk):
        s = slice(i * DH, (i + 1) * DH)
        dkv_out[i][:, :DH] += dk[s]
        dkv_out[i][:, DH:] += dv[s]
    r = dot(ds_hi, kc[:, : 2 * DH], TN)
    dq = (r[:, :DH] + r[:, DH:] + dot(ds_lo, kc[:, :DH], TN)) * (1.0 / math.sqrt(DH))
    for g in range(nq):
        t = dq[g * DH : (g + 1) * DH]
        dq_out[g][...] = dq_in[g][...] + t if has_dq else t


def grads(rank, order, packs, groups, blocks, dq=None, dkv=None):
    offsets = list(blocks)
    pieces = [piece for o in offsets for piece in blocks[o]]
    nq, nk = len(packs), len(offsets)
    rows = packs[0].shape[0]
    whole = lambda a: pl.BlockSpec(a.shape, lambda h: (0, 0))
    head = lambda first: pl.BlockSpec((rows, DH), lambda h: (0, first + h))
    scalar = pl.BlockSpec(memory_space=pltpu.SMEM)
    in_specs = [scalar, scalar]
    in_specs += [head(0)] * nq + [head(HQ)] * nq + [pl.BlockSpec((rows, DH), lambda h: (0, 2 * HQ))] * nq
    in_specs += [whole(p) for p in pieces]
    args = [rank, order, *packs, *packs, *packs, *pieces]
    aliases = {}
    if dq is not None:
        for g in range(nq):
            aliases[len(args) + g] = g
        in_specs += [head(0)] * nq
        args += dq
    if dkv is not None:
        for i in range(nk):
            aliases[len(args) + i] = nq + i
        in_specs += [pl.BlockSpec((rows, 2 * DH), lambda h: (0, 0))] * nk
        args += [dkv[o] for o in offsets]
    out_specs = [head(0)] * nq + [pl.BlockSpec((rows, 2 * DH), lambda h: (0, 0))] * nk
    out_shape = [jax.ShapeDtypeStruct((rows, HQ * DH), F32)] * nq + [jax.ShapeDtypeStruct((rows, 2 * DH), F32)] * nk
    keys, queries = nk * rows, nq * rows
    diag = 0 in offsets and groups[0] == (0, 0)
    outs = pl.pallas_call(
        functools.partial(grads_kernel, offsets, groups, diag, len(pieces), dq is not None, dkv is not None),
        grid=(HQ,),
        in_specs=in_specs,
        out_specs=out_specs,
        out_shape=out_shape,
        input_output_aliases=aliases,
        scratch_shapes=[pltpu.VMEM((keys, 4 * DH), BF16)] * 2 + [pltpu.VMEM((queries, 4 * DH), BF16)] * 2,
        compiler_params=pltpu.CompilerParams(vmem_limit_bytes=40 * 2**20),
        cost_estimate=pl.CostEstimate(
            flops=HQ * keys * queries * DH * 2 * 20, bytes_accessed=2**21, transcendentals=HQ * keys * queries
        ),
        name="grads",
    )(*args)
    return outs[:nq], dict(zip(offsets, outs[nq:]))


def local(query, key, value, output, grad_output, lse, span_order):
    rows = key.shape[0]
    rank = lax.axis_index("ctx").astype(jnp.int32).reshape(1)
    pack = pl.pallas_call(
        pack_kernel,
        out_shape=jax.ShapeDtypeStruct((rows, (2 * HQ + 1) * DH), F32),
        compiler_params=pltpu.CompilerParams(vmem_limit_bytes=32 * 2**20),
        name="pack",
    )(query, grad_output, output, lse)
    kv = jnp.concatenate([key, value], axis=1)
    half = rows // 2

    pack_x = send(pack, dx=1)
    pack_c = send(pack, dc=1)
    f1, b1 = send(kv, dz=1), send(kv, dz=-1)
    f2, b2 = send(f1, dz=1), send(b1, dz=-1)
    f3, b3 = send(f2, dz=1), send(b2, dz=-1)
    f4, b4 = send(f3[:half], dz=1), send(b3[half:], dz=-1)
    pack_xc = send(pack_x, dc=1)
    near = {0: [kv], -1: [f1], 1: [b1], -2: [f2], 2: [b2]}
    far = {-3: [f3], 3: [b3], 4: [f4, b4]}
    own, other = [(0, 0), (0, 1)], [(1, 0), (1, 1)]

    dq_own, dkv_near = grads(rank, span_order, [pack, pack_c], own, near)
    dq_own, dkv_far = grads(rank, span_order, [pack, pack_c], own, far, dq=dq_own)
    dq_other, dkv_far = grads(rank, span_order, [pack_x, pack_xc], other, far, dkv=dkv_far)
    dq_other, dkv_near = grads(rank, span_order, [pack_x, pack_xc], other, near, dq=dq_other, dkv=dkv_near)

    f, b = send(dkv_far[4][:half], dz=1), send(dkv_far[4][half:], dz=-1)
    f = send(dkv_far[3].at[:half].add(f), dz=1)
    b = send(dkv_far[-3].at[half:].add(b), dz=-1)
    f, b = send(f + dkv_near[2], dz=1), send(b + dkv_near[-2], dz=-1)
    f, b = send(f + dkv_near[1], dz=1), send(b + dkv_near[-1], dz=-1)
    dkv = dkv_near[0] + f + b

    dq = dq_own[0] + send(dq_own[1], dc=1)
    dq = dq + send(dq_other[0] + send(dq_other[1], dc=1), dx=1)
    return dq, dkv[:, :DH], dkv[:, DH:]


def solution(mesh):
    in_specs = (
        P("ctx", "heads"),
        P("ctx", "heads"),
        P("ctx", "heads"),
        P("ctx", "heads"),
        P("ctx", "heads"),
        P("heads", "ctx"),
        P("heads"),
    )
    out_specs = (P("ctx", "heads"), P("ctx", "heads"), P("ctx", "heads"))
    return jax.shard_map(local, mesh=mesh, in_specs=in_specs, out_specs=out_specs, check_vma=False)
```

```python
import functools
import math

import jax
import jax.numpy as jnp
from jax import lax
from jax.experimental import pallas as pl
from jax.experimental.pallas import tpu as pltpu
from jax.sharding import PartitionSpec as P

ZS = 8
DH = 128
HQ = 8
CHUNK = 4
HALF = 64
LOG2E = 1.4426950408889634
BIG = 1e30
F32 = jnp.float32
BF16 = jnp.bfloat16
PACK_VMEM = 24
NT = (((1,), (1,)), ((), ()))
NN = (((1,), (0,)), ((), ()))
TN = (((0,), (0,)), ((), ()))
VM = pl.BlockSpec(memory_space=pltpu.VMEM)
SM = pl.BlockSpec(memory_space=pltpu.SMEM)


def send(x, to, back=False):
    perm = []
    for z in range(ZS):
        for xh in range(2):
            for c in range(2):
                tz, tx, tc = to(z, xh, c)
                perm.append((z * 4 + xh * 2 + c, (tz % ZS) * 4 + tx * 2 + tc))
    return lax.ppermute(x, "ctx", [(b, a) for a, b in perm] if back else perm)


def core(z, xh, c):
    return z, xh, 1 - c


def ring(z, xh, c):
    return z + 1 - 2 * c, xh, c


def chip(z, xh, c):
    return z, 1 - xh, c ^ xh


def across(z, xh, c):
    return z + ZS // 2, xh, c


def split(x):
    hi = x.astype(BF16)
    return hi, (x - hi.astype(F32)).astype(BF16)


def dot(a, b, dims=NN):
    return lax.dot_general(a, b, dims, preferred_element_type=F32)


def pack_kernel(rank_ref, order_ref, q_hbm, do_hbm, o_hbm, lse_hbm, p_ref, q, do, o, lse_ref, sems):
    copies = [
        pltpu.make_async_copy(do_hbm, do, sems.at[0]),
        pltpu.make_async_copy(o_hbm, o, sems.at[1]),
        pltpu.make_async_copy(q_hbm, q, sems.at[2]),
        pltpu.make_async_copy(lse_hbm, lse_ref, sems.at[3]),
    ]
    for copy in copies:
        copy.start()
    rows = q.shape[0]
    lane = lax.broadcasted_iota(jnp.int32, (rows, DH), 1)
    row = lax.broadcasted_iota(jnp.int32, (rows, DH), 0)
    slot = rank_ref[0] * 2
    pos = jnp.where(row < HALF, order_ref[slot], order_ref[slot + 1])
    x = jnp.where((lane < HALF) & (lane > pos), -BIG, 0.0)

    def put(into, column, first):
        hi = column.astype(BF16).astype(F32)
        mid = (column - hi).astype(BF16).astype(F32)
        lo = column - hi - mid
        at = lane - first
        return jnp.where(at == 0, hi, jnp.where(at == 1, mid, jnp.where(at == 2, lo, into)))

    copies[3].wait()
    lse = jnp.concatenate([lse_ref[...] * (-LOG2E), jnp.zeros((DH - HQ, rows), F32)], axis=0).T
    for h in range(HQ):
        x = put(x, jnp.sum(jnp.where(lane == h, lse, 0.0), axis=1, keepdims=True), HALF + 3 * h)
    copies[0].wait()
    copies[1].wait()
    for h in range(HQ):
        s = slice(h * DH, (h + 1) * DH)
        x = put(x, -jnp.sum(do[:, s] * o[:, s], axis=1, keepdims=True), HALF + 3 * (HQ + h))
    w = HQ * DH
    p_ref[:, w : 2 * w] = do[...]
    p_ref[:, 2 * w :] = x
    copies[2].wait()
    p_ref[:, :w] = q[...] * (LOG2E / math.sqrt(DH))


def pack(rank, order, query, grad_output, output, lse):
    rows = query.shape[0]
    hbm = pl.BlockSpec(memory_space=pltpu.HBM)
    return pl.pallas_call(
        pack_kernel,
        in_specs=[SM, SM, hbm, hbm, hbm, hbm],
        out_specs=VM,
        out_shape=jax.ShapeDtypeStruct((rows, (2 * HQ + 1) * DH), F32),
        scratch_shapes=[pltpu.VMEM((rows, HQ * DH), F32)] * 3
        + [pltpu.VMEM((HQ, rows), F32), pltpu.SemaphoreType.DMA((4,))],
        compiler_params=pltpu.CompilerParams(vmem_limit_bytes=PACK_VMEM * 2**20),
        cost_estimate=pl.CostEstimate(flops=2**32, bytes_accessed=2**21, transcendentals=0),
        name="pack",
    )(rank, *[pltpu.with_memory_space_constraint(x, pltpu.HBM) for x in (order, query, grad_output, output, lse)])


def half_kernel(rank_ref, b_ref, out_ref):
    first = pl.multiple_of((rank_ref[0] % 2) * HALF, HALF)
    out_ref[:HALF] = b_ref[pl.ds(first, HALF)]
    out_ref[HALF:] = b_ref[pl.ds(first + 2 * HALF, HALF)]


def join_kernel(rank_ref, r_ref, r4_ref, later_ref, mine_ref, other_ref):
    first = pl.multiple_of((rank_ref[0] % 2) * HALF, HALF)
    mine_ref[...] = r_ref[: 2 * HALF]
    other_ref[...] = r_ref[2 * HALF :]
    mine_ref[pl.ds(first, HALF)] += r4_ref[:HALF]
    other_ref[pl.ds(first, HALF)] += r4_ref[HALF:]


def small(kernel, n, *args):
    shape = jax.ShapeDtypeStruct((2 * HALF, 2 * DH), F32)
    return pl.pallas_call(
        kernel,
        in_specs=[SM] + [VM if a.shape[1] == 2 * DH else pl.BlockSpec(memory_space=pl.ANY) for a in args[1:]],
        out_specs=[VM] * n,
        out_shape=[shape] * n,
        compiler_params=pltpu.CompilerParams(vmem_limit_bytes=4 * 2**20),
        name=kernel.__name__,
    )(*args)


def tie_kernel(x_ref, sign_ref, out_ref):
    pass


def grads_kernel(steps, pairs, has_dq, has_dkv, ties, *refs):
    refs = list(refs)
    take = lambda n: [refs.pop(0) for _ in range(n)]
    rank_ref, order_ref = take(2)
    groups = sum(pairs, ())
    packs = dict(zip(groups, take(len(groups))))
    kv_refs = take(len(steps))
    dq_in = dict(zip(has_dq, take(len(has_dq))))
    dkv_in = dict(zip(has_dkv, take(len(has_dkv))))
    take(ties)
    dq_out = dict(zip(groups, take(len(groups))))
    dkv_out = take(len(steps))
    sign = refs.pop(0)
    sign[...] = jnp.zeros_like(sign)
    kc, vc = take(2)

    rank = rank_ref[0]
    z, xh, c = rank // 4, (rank // 2) % 2, rank % 2
    lane = lax.broadcasted_iota(jnp.int32, (HALF, DH), 1)
    at = 0
    for step, ref in zip(steps, kv_refs):
        zk = lax.rem(z + (2 * c - 1) * step + ZS, ZS)
        for i in range(ref.shape[0] // HALF):
            if step < ZS // 2:
                line, part = (c if i < 2 else 1 - c), i % 2
            else:
                line, part = (c if i < 1 else 1 - c), c
            pos = order_ref[(zk * 4 + xh * 2 + line) * 2 + part]
            hot = jnp.where((lane == pos) | (lane >= HALF), 1.0, 0.0).astype(BF16)
            s, to = slice(i * HALF, (i + 1) * HALF), slice(at, at + HALF)
            hi, lo = split(ref[s, :DH])
            kc[to, :] = jnp.concatenate([hi, lo, hi, hot], axis=1)
            hi, lo = split(ref[s, DH:])
            vc[to, :] = jnp.concatenate([hi, lo, hi, hot], axis=1)
            at += HALF

    lane = lax.broadcasted_iota(jnp.int32, (DH, DH), 1)
    first = True
    for gs, half in ((gs, half) for gs in pairs for half in range(HQ // CHUNK)):
        qs, ds = [], []
        for h in range(CHUNK):
            head = half * CHUNK + h
            mine = (lane < HALF) | ((lane - HALF) // 3 == head)
            mine_do = (lane - HALF) // 3 == HQ + head
            for g in gs:
                ref = packs[g]
                terms = ref[:, 2 * HQ * DH :]
                q_at, do_at = head * DH, (HQ + head) * DH
                hi, lo = split(ref[:, q_at : q_at + DH])
                bias = jnp.where(mine, terms, 0.0).astype(BF16)
                qs.append(jnp.concatenate([hi, hi, lo, bias], axis=1))
                hi, lo = split(ref[:, do_at : do_at + DH])
                bias = jnp.where(mine_do, terms, 0.0).astype(BF16)
                ds.append(jnp.concatenate([hi, hi, lo, bias], axis=1))
        qc, dc = jnp.concatenate(qs, axis=0), jnp.concatenate(ds, axis=0)
        p = jnp.exp2(dot(kc[...], qc, NT))
        if 0 in steps and "self" in gs:
            top = p[:DH]
            a = lax.broadcasted_iota(jnp.int32, top.shape, 0)
            b = lax.broadcasted_iota(jnp.int32, top.shape, 1)
            rows = len(gs) * DH
            b = b - (b // rows) * rows - gs.index("self") * DH
            top = jnp.where((b >= 0) & (b < DH) & (a // HALF == b // HALF) & (a > b), 0.0, top)
            p = top if p.shape[0] == DH else jnp.concatenate([top, p[DH:]], axis=0)
        d = p * dot(vc[...], dc, NT)
        p_hi, p_lo = split(p)
        r = dot(p_hi, dc[:, DH : 3 * DH])
        dv = r[:, :DH] + r[:, DH:] + dot(p_lo, dc[:, :DH])
        d_hi, d_lo = split(d)
        r = dot(d_hi, qc[:, DH : 3 * DH])
        dk = (r[:, :DH] + r[:, DH:] + dot(d_lo, qc[:, :DH])) * (1.0 / LOG2E)
        at = 0
        for step, out in zip(steps, dkv_out):
            s = slice(at, at + out.shape[0])
            at += out.shape[0]
            if first:
                out[:, :DH] = dkv_in[step][:, :DH] + dk[s] if step in dkv_in else dk[s]
                out[:, DH:] = dkv_in[step][:, DH:] + dv[s] if step in dkv_in else dv[s]
            else:
                out[:, :DH] += dk[s]
                out[:, DH:] += dv[s]
        first = False
        r = dot(d_hi, kc[:, : 2 * DH], TN)
        dq = (r[:, :DH] + r[:, DH:] + dot(d_lo, kc[:, :DH], TN)) * (1.0 / math.sqrt(DH))
        for h in range(CHUNK):
            for j, g in enumerate(gs):
                s = slice((half * CHUNK + h) * DH, (half * CHUNK + h + 1) * DH)
                t = dq[(h * len(gs) + j) * DH : (h * len(gs) + j + 1) * DH]
                dq_out[g][:, s] = dq_in[g][:, s] + t if g in dq_in else t


class Totals:
    def __init__(self, rank, order, packs, blocks):
        self.rank, self.order, self.packs, self.blocks = rank, order, packs, blocks
        self.dq, self.dkv, self.last = {}, {}, None

    def after(self, x):
        any_ = pl.BlockSpec(memory_space=pl.ANY)
        return pl.pallas_call(
            tie_kernel,
            in_specs=[any_, any_],
            out_specs=any_,
            out_shape=jax.ShapeDtypeStruct(x.shape, x.dtype),
            input_output_aliases={0: 0},
            compiler_params=pltpu.CompilerParams(vmem_limit_bytes=2**20),
            name="tie",
        )(x, self.last)

    def add(self, steps, *pairs, need=()):
        groups = sum(pairs, ())
        args = [self.packs[g] for g in groups] + [self.blocks[s] for s in steps]
        has_dq = [g for g in groups if g in self.dq]
        has_dkv = [s for s in steps if s in self.dkv]
        aliases = {}
        for g in has_dq:
            aliases[2 + len(args)] = groups.index(g)
            args.append(self.dq[g])
        for s in has_dkv:
            aliases[2 + len(args)] = len(groups) + steps.index(s)
            args.append(self.dkv[s])
        ties = [*need] if self.last is None else [self.last, *need]
        args += ties
        rows = [self.blocks[s].shape[0] for s in steps]
        keys = sum(rows)
        outs = pl.pallas_call(
            functools.partial(grads_kernel, steps, pairs, has_dq, has_dkv, len(ties)),
            in_specs=[SM, SM] + [VM] * (len(args) - len(ties)) + [pl.BlockSpec(memory_space=pl.ANY)] * len(ties),
            out_specs=[VM] * (len(groups) + len(steps) + 1),
            out_shape=[jax.ShapeDtypeStruct((DH, HQ * DH), F32)] * len(groups)
            + [jax.ShapeDtypeStruct((n, 2 * DH), F32) for n in rows]
            + [jax.ShapeDtypeStruct((8, DH), F32)],
            input_output_aliases=aliases,
            scratch_shapes=[pltpu.VMEM((keys, 4 * DH), BF16)] * 2,
            compiler_params=pltpu.CompilerParams(vmem_limit_bytes=(8 + keys // 40) * 2**20),
            cost_estimate=pl.CostEstimate(flops=2**10, bytes_accessed=2**10, transcendentals=0),
            name="grads_" + "".join(map(str, steps)) + "_" + "".join(g[0] for g in groups),
        )(self.rank, self.order, *args)
        self.dq.update(zip(groups, outs))
        self.dkv.update(zip(steps, outs[len(groups) : -1]))
        self.last = outs[-1]


def local(query, key, value, output, grad_output, lse, span_order):
    rank = lax.axis_index("ctx").astype(jnp.int32).reshape(1)
    c = rank[0] % 2
    kv = jnp.concatenate([key, value], axis=1)
    kv_c = send(kv, core)
    p = pack(rank, span_order, query, grad_output, output, lse)
    packs = {"self": p, "x": send(p, chip), "core": send(p, core)}
    blocks = {0: kv}
    total = Totals(rank, span_order, packs, blocks)
    own, other = ("self", "core"), ("x", "v")
    blocks[1] = send(jnp.concatenate([kv, kv_c], axis=0), ring)
    total.add([0], own)
    blocks[1] = total.after(blocks[1])
    blocks[2] = send(blocks[1], ring)
    total.add([1], own)
    blocks[2] = total.after(blocks[2])
    blocks[3] = send(blocks[2], ring)
    total.add([2], own)
    total.add([3], own)
    blocks[4] = send(total.after(small(half_kernel, 1, rank, blocks[3])[0]), ring)
    packs["x"] = total.after(packs["x"])
    packs["v"] = send(packs["x"], core)
    total.add([3], other)
    r = send(total.dkv[3], ring, back=True)
    total.add([2], other)
    total.add([0, 1, 4], other, need=[r])
    r = send(total.dkv[2] + r, ring, back=True)
    dq_x = total.dq["x"] + send(total.dq["v"], core)
    dq_x = send(dq_x, chip, back=True)
    total.add([4], own)
    r4 = send(total.dkv[4], across)
    r = send(total.dkv[1] + r, ring, back=True)
    r, r_c = small(join_kernel, 2, rank, r, r4, dq_x)
    dkv = total.dkv[0] + r + send(r_c, core)
    dq = total.dq["self"] + send(total.dq["core"], core) + dq_x
    return dq, dkv[:, :DH], dkv[:, DH:]


def solution(mesh):
    in_specs = (
        P("ctx", "heads"),
        P("ctx", "heads"),
        P("ctx", "heads"),
        P("ctx", "heads"),
        P("ctx", "heads"),
        P("heads", "ctx"),
        P("heads"),
    )
    out_specs = (P("ctx", "heads"), P("ctx", "heads"), P("ctx", "heads"))
    return jax.shard_map(local, mesh=mesh, in_specs=in_specs, out_specs=out_specs, check_vma=False)
```

```python
import functools
import math

import jax
import jax.numpy as jnp
from jax import lax
from jax.experimental import pallas as pl
from jax.experimental.pallas import tpu as pltpu
from jax.sharding import PartitionSpec as P

ZS = 8
DH = 128
HQ = 8
CHUNK = 4
HALF = 64
LOG2E = 1.4426950408889634
BIG = 1e30
F32 = jnp.float32
BF16 = jnp.bfloat16
PACK_VMEM = 24
NT = (((1,), (1,)), ((), ()))
NN = (((1,), (0,)), ((), ()))
TN = (((0,), (0,)), ((), ()))
VM = pl.BlockSpec(memory_space=pltpu.VMEM)
SM = pl.BlockSpec(memory_space=pltpu.SMEM)


def send(x, to, back=False):
    perm = []
    for z in range(ZS):
        for xh in range(2):
            for c in range(2):
                tz, tx, tc = to(z, xh, c)
                perm.append((z * 4 + xh * 2 + c, (tz % ZS) * 4 + tx * 2 + tc))
    return lax.ppermute(x, "ctx", [(b, a) for a, b in perm] if back else perm)


def core(z, xh, c):
    return z, xh, 1 - c


def ring(z, xh, c):
    return z + 1 - 2 * c, xh, c


def chip(z, xh, c):
    return z, 1 - xh, c ^ xh


def across(z, xh, c):
    return z + ZS // 2, xh, c


def split(x):
    hi = x.astype(BF16)
    return hi, (x - hi.astype(F32)).astype(BF16)


def dot(a, b, dims=NN):
    return lax.dot_general(a, b, dims, preferred_element_type=F32)


def pack_kernel(rank_ref, order_ref, q_hbm, do_hbm, o_hbm, lse_hbm, p_ref, a_ref, b_ref, q, do, o, lse_ref, sems):
    copies = [
        pltpu.make_async_copy(do_hbm, do, sems.at[0]),
        pltpu.make_async_copy(o_hbm, o, sems.at[1]),
        pltpu.make_async_copy(q_hbm, q, sems.at[2]),
        pltpu.make_async_copy(lse_hbm, lse_ref, sems.at[3]),
    ]
    for copy in copies:
        copy.start()
    rows = q.shape[0]
    lane = lax.broadcasted_iota(jnp.int32, (rows, DH), 1)
    row = lax.broadcasted_iota(jnp.int32, (rows, DH), 0)
    slot = rank_ref[0] * 2
    pos = jnp.where(row < HALF, order_ref[slot], order_ref[slot + 1])
    x = jnp.where((lane < HALF) & (lane > pos), -BIG, 0.0)

    def put(into, column, first):
        hi = column.astype(BF16).astype(F32)
        mid = (column - hi).astype(BF16).astype(F32)
        lo = column - hi - mid
        at = lane - first
        return jnp.where(at == 0, hi, jnp.where(at == 1, mid, jnp.where(at == 2, lo, into)))

    copies[3].wait()
    lse = jnp.concatenate([lse_ref[...] * (-LOG2E), jnp.zeros((DH - HQ, rows), F32)], axis=0).T
    for h in range(HQ):
        x = put(x, jnp.sum(jnp.where(lane == h, lse, 0.0), axis=1, keepdims=True), HALF + 3 * h)
    copies[0].wait()
    copies[1].wait()
    for h in range(HQ):
        s = slice(h * DH, (h + 1) * DH)
        x = put(x, -jnp.sum(do[:, s] * o[:, s], axis=1, keepdims=True), HALF + 3 * (HQ + h))
    w = CHUNK * DH
    p_ref[:, 2 * w : 4 * w] = do[...]
    a_ref[:, w : 2 * w] = do[:, :w]
    b_ref[:, w:] = do[:, w:]
    p_ref[:, 4 * w :] = x
    a_ref[:, 2 * w :] = x
    copies[2].wait()
    scaled = q[...] * (LOG2E / math.sqrt(DH))
    p_ref[:, : 2 * w] = scaled
    a_ref[:, :w] = scaled[:, :w]
    b_ref[:, :w] = scaled[:, w:]


def pack(rank, order, query, grad_output, output, lse):
    rows = query.shape[0]
    hbm = pl.BlockSpec(memory_space=pltpu.HBM)
    return pl.pallas_call(
        pack_kernel,
        in_specs=[SM, SM, hbm, hbm, hbm, hbm],
        out_specs=[VM] * 3,
        out_shape=[jax.ShapeDtypeStruct((rows, n * DH), F32) for n in (2 * HQ + 1, HQ + 1, HQ)],
        scratch_shapes=[pltpu.VMEM((rows, HQ * DH), F32)] * 3
        + [pltpu.VMEM((HQ, rows), F32), pltpu.SemaphoreType.DMA((4,))],
        compiler_params=pltpu.CompilerParams(vmem_limit_bytes=PACK_VMEM * 2**20),
        cost_estimate=pl.CostEstimate(flops=2**32, bytes_accessed=2**21, transcendentals=0),
        name="pack",
    )(rank, *[pltpu.with_memory_space_constraint(x, pltpu.HBM) for x in (order, query, grad_output, output, lse)])


def half_kernel(rank_ref, b_ref, out_ref):
    first = pl.multiple_of((rank_ref[0] % 2) * HALF, HALF)
    out_ref[:HALF] = b_ref[pl.ds(first, HALF)]
    out_ref[HALF:] = b_ref[pl.ds(first + 2 * HALF, HALF)]


def join_kernel(rank_ref, r_ref, r4_ref, later_ref, mine_ref, other_ref):
    first = pl.multiple_of((rank_ref[0] % 2) * HALF, HALF)
    mine_ref[...] = r_ref[: 2 * HALF]
    other_ref[...] = r_ref[2 * HALF :]
    mine_ref[pl.ds(first, HALF)] += r4_ref[:HALF]
    other_ref[pl.ds(first, HALF)] += r4_ref[HALF:]


def small(kernel, n, *args):
    shape = jax.ShapeDtypeStruct((2 * HALF, 2 * DH), F32)
    return pl.pallas_call(
        kernel,
        in_specs=[SM] + [VM if a.shape[1] == 2 * DH else pl.BlockSpec(memory_space=pl.ANY) for a in args[1:]],
        out_specs=[VM] * n,
        out_shape=[shape] * n,
        compiler_params=pltpu.CompilerParams(vmem_limit_bytes=4 * 2**20),
        name=kernel.__name__,
    )(*args)


def tie_kernel(x_ref, sign_ref, out_ref):
    pass


def names_of(jobs):
    names = []
    for gs, halves in jobs:
        for g in gs:
            names += [(g, None)] if g in ("self", "core") else [(g, half) for half in (0, *halves)]
    return list(dict.fromkeys(names))


def grads_kernel(steps, jobs, dq_from, dq_old, has_dkv, ties, *refs):
    refs = list(refs)
    take = lambda n: [refs.pop(0) for _ in range(n)]
    rank_ref, order_ref = take(2)
    groups = list(dict.fromkeys(g for gs, _ in jobs for g in gs))
    names = names_of(jobs)
    packs = dict(zip(names, take(len(names))))
    kv_refs = take(len(steps))
    dq_in = dict(zip(dq_from, take(len(dq_from))))
    dkv_in = dict(zip(has_dkv, take(len(has_dkv))))
    take(ties)
    dq_out = dict(zip(groups, take(len(groups))))
    dkv_out = take(len(steps))
    sign = refs.pop(0)
    sign[...] = jnp.zeros_like(sign)
    kc, vc = take(2)

    rank = rank_ref[0]
    z, xh, c = rank // 4, (rank // 2) % 2, rank % 2
    lane = lax.broadcasted_iota(jnp.int32, (HALF, DH), 1)
    at = 0
    for step, ref in zip(steps, kv_refs):
        zk = lax.rem(z + (2 * c - 1) * step + ZS, ZS)
        for i in range(ref.shape[0] // HALF):
            if step < ZS // 2:
                line, part = (c if i < 2 else 1 - c), i % 2
            else:
                line, part = (c if i < 1 else 1 - c), c
            pos = order_ref[(zk * 4 + xh * 2 + line) * 2 + part]
            hot = jnp.where((lane == pos) | (lane >= HALF), 1.0, 0.0).astype(BF16)
            s, to = slice(i * HALF, (i + 1) * HALF), slice(at, at + HALF)
            hi, lo = split(ref[s, :DH])
            kc[to, :] = jnp.concatenate([hi, lo, hi, hot], axis=1)
            hi, lo = split(ref[s, DH:])
            vc[to, :] = jnp.concatenate([hi, lo, hi, hot], axis=1)
            at += HALF

    lane = lax.broadcasted_iota(jnp.int32, (DH, DH), 1)
    first = True
    for gs, half in ((gs, half) for gs, halves in jobs for half in halves):
        qs, ds = [], []
        for h in range(CHUNK):
            head = half * CHUNK + h
            mine = (lane < HALF) | ((lane - HALF) // 3 == head)
            mine_do = (lane - HALF) // 3 == HQ + head
            for g in gs:
                if (g, None) in packs:
                    ref, q_at, do_at = packs[g, None], head * DH, (HQ + head) * DH
                    terms = ref[:, 2 * HQ * DH :]
                else:
                    ref, q_at, do_at = packs[g, half], h * DH, (CHUNK + h) * DH
                    terms = packs[g, 0][:, 2 * CHUNK * DH :]
                hi, lo = split(ref[:, q_at : q_at + DH])
                bias = jnp.where(mine, terms, 0.0).astype(BF16)
                qs.append(jnp.concatenate([hi, hi, lo, bias], axis=1))
                hi, lo = split(ref[:, do_at : do_at + DH])
                bias = jnp.where(mine_do, terms, 0.0).astype(BF16)
                ds.append(jnp.concatenate([hi, hi, lo, bias], axis=1))
        qc, dc = jnp.concatenate(qs, axis=0), jnp.concatenate(ds, axis=0)
        p = jnp.exp2(dot(kc[...], qc, NT))
        if 0 in steps and "self" in gs:
            top = p[:DH]
            a = lax.broadcasted_iota(jnp.int32, top.shape, 0)
            b = lax.broadcasted_iota(jnp.int32, top.shape, 1)
            rows = len(gs) * DH
            b = b - (b // rows) * rows - gs.index("self") * DH
            top = jnp.where((b >= 0) & (b < DH) & (a // HALF == b // HALF) & (a > b), 0.0, top)
            p = top if p.shape[0] == DH else jnp.concatenate([top, p[DH:]], axis=0)
        d = p * dot(vc[...], dc, NT)
        p_hi, p_lo = split(p)
        r = dot(p_hi, dc[:, DH : 3 * DH])
        dv = r[:, :DH] + r[:, DH:] + dot(p_lo, dc[:, :DH])
        d_hi, d_lo = split(d)
        r = dot(d_hi, qc[:, DH : 3 * DH])
        dk = (r[:, :DH] + r[:, DH:] + dot(d_lo, qc[:, :DH])) * (1.0 / LOG2E)
        at = 0
        for step, out in zip(steps, dkv_out):
            s = slice(at, at + out.shape[0])
            at += out.shape[0]
            if first:
                out[:, :DH] = dkv_in[step][:, :DH] + dk[s] if step in dkv_in else dk[s]
                out[:, DH:] = dkv_in[step][:, DH:] + dv[s] if step in dkv_in else dv[s]
            else:
                out[:, :DH] += dk[s]
                out[:, DH:] += dv[s]
        first = False
        r = dot(d_hi, kc[:, : 2 * DH], TN)
        dq = (r[:, :DH] + r[:, DH:] + dot(d_lo, kc[:, :DH], TN)) * (1.0 / math.sqrt(DH))
        for h in range(CHUNK):
            for j, g in enumerate(gs):
                s = slice((half * CHUNK + h) * DH, (half * CHUNK + h + 1) * DH)
                t = dq[(h * len(gs) + j) * DH : (h * len(gs) + j + 1) * DH]
                dq_out[g][:, s] = dq_in[g][:, s] + t if (g, half) in dq_old else t


class Totals:
    def __init__(self, rank, order, packs, blocks):
        self.rank, self.order, self.packs, self.blocks = rank, order, packs, blocks
        self.dq, self.held, self.dkv, self.last = {}, set(), {}, None

    def after(self, x):
        any_ = pl.BlockSpec(memory_space=pl.ANY)
        return pl.pallas_call(
            tie_kernel,
            in_specs=[any_, any_],
            out_specs=any_,
            out_shape=jax.ShapeDtypeStruct(x.shape, x.dtype),
            input_output_aliases={0: 0},
            compiler_params=pltpu.CompilerParams(vmem_limit_bytes=2**20),
            name="tie",
        )(x, self.last)

    def add(self, steps, *jobs, need=(), flops=2**10):
        groups = list(dict.fromkeys(g for gs, _ in jobs for g in gs))
        args = [self.packs[n] for n in names_of(jobs)] + [self.blocks[s] for s in steps]
        dq_from = [g for g in groups if g in self.dq]
        dq_old = frozenset(self.held)
        self.held.update((g, half) for gs, halves in jobs for g in gs for half in halves)
        has_dkv = [s for s in steps if s in self.dkv]
        aliases = {}
        for g in dq_from:
            aliases[2 + len(args)] = groups.index(g)
            args.append(self.dq[g])
        for s in has_dkv:
            aliases[2 + len(args)] = len(groups) + steps.index(s)
            args.append(self.dkv[s])
        ties = [*need] if self.last is None else [self.last, *need]
        args += ties
        rows = [self.blocks[s].shape[0] for s in steps]
        keys = sum(rows)
        outs = pl.pallas_call(
            functools.partial(grads_kernel, steps, jobs, dq_from, dq_old, has_dkv, len(ties)),
            in_specs=[SM, SM] + [VM] * (len(args) - len(ties)) + [pl.BlockSpec(memory_space=pl.ANY)] * len(ties),
            out_specs=[VM] * (len(groups) + len(steps) + 1),
            out_shape=[jax.ShapeDtypeStruct((DH, HQ * DH), F32)] * len(groups)
            + [jax.ShapeDtypeStruct((n, 2 * DH), F32) for n in rows]
            + [jax.ShapeDtypeStruct((8, DH), F32)],
            input_output_aliases=aliases,
            scratch_shapes=[pltpu.VMEM((keys, 4 * DH), BF16)] * 2,
            compiler_params=pltpu.CompilerParams(vmem_limit_bytes=(8 + keys // 40) * 2**20),
            cost_estimate=pl.CostEstimate(flops=flops, bytes_accessed=2**10, transcendentals=0),
            name="grads_" + "".join(map(str, steps)) + "_" + "_".join(gs[0] + "ab"[halves[0] : halves[-1] + 1] for gs, halves in jobs),
        )(self.rank, self.order, *args)
        self.dq.update(zip(groups, outs))
        self.dkv.update(zip(steps, outs[len(groups) : -1]))
        self.last = outs[-1]


def local(query, key, value, output, grad_output, lse, span_order):
    rank = lax.axis_index("ctx").astype(jnp.int32).reshape(1)
    c = rank[0] % 2
    kv = jnp.concatenate([key, value], axis=1)
    kv_c = send(kv, core)
    p, pa, pb = pack(rank, span_order, query, grad_output, output, lse)
    packs = {("self", None): p, ("x", 0): send(pa, chip), ("core", None): send(p, core)}
    blocks = {0: kv}
    total = Totals(rank, span_order, packs, blocks)
    after = total.after
    own, other = ("self", "core"), ("x", "v")
    both = (0, 1)
    blocks[1] = send(jnp.concatenate([kv, kv_c], axis=0), ring)
    total.add([0], (own, both))
    blocks[1] = after(blocks[1])
    blocks[2] = send(blocks[1], ring)
    total.add([1], (own, both))
    packs["x", 0] = after(packs["x", 0])
    packs["v", 0] = send(packs["x", 0], core)
    packs["x", 1] = send(after(pb), chip)
    blocks[2] = after(blocks[2])
    blocks[3] = send(blocks[2], ring)
    total.add([2], (own, both), flops=2**37)
    total.add([0, 1, 2], (other, (0,)))
    blocks[3] = after(blocks[3])
    blocks[4] = send(small(half_kernel, 1, rank, blocks[3])[0], ring)
    total.add([3], (own, both))
    packs["x", 1] = after(packs["x", 1])
    packs["v", 1] = send(packs["x", 1], core)
    total.add([3], (other, (0,)), need=[blocks[4]], flops=2**37)
    total.add([3], (other, (1,)))
    r = send(total.dkv[3], ring, back=True)
    total.add([4], (other, both), (own, both), flops=2**37)
    total.add([0, 1, 2], (other, (1,)), need=[r])
    r = send(total.dkv[2] + r, ring, back=True)
    dq_x = total.dq["x"] + send(total.dq["v"], core)
    dq_x = send(dq_x, chip, back=True)
    r4 = send(total.dkv[4], across)
    r = send(total.dkv[1] + r, ring, back=True)
    r, r_c = small(join_kernel, 2, rank, r, r4, dq_x)
    dkv = total.dkv[0] + r + send(r_c, core)
    dq = total.dq["self"] + send(total.dq["core"], core) + dq_x
    return dq, dkv[:, :DH], dkv[:, DH:]


def solution(mesh):
    in_specs = (
        P("ctx", "heads"),
        P("ctx", "heads"),
        P("ctx", "heads"),
        P("ctx", "heads"),
        P("ctx", "heads"),
        P("heads", "ctx"),
        P("heads"),
    )
    out_specs = (P("ctx", "heads"), P("ctx", "heads"), P("ctx", "heads"))
    return jax.shard_map(local, mesh=mesh, in_specs=in_specs, out_specs=out_specs, check_vma=False)
```

```python
import functools
import math

import jax
import jax.numpy as jnp
from jax import lax
from jax.experimental import pallas as pl
from jax.experimental.pallas import tpu as pltpu
from jax.sharding import PartitionSpec as P

ZS = 8
DH = 128
HQ = 8
CHUNK = 4
HALF = 64
LOG2E = 1.4426950408889634
BIG = 1e30
F32 = jnp.float32
BF16 = jnp.bfloat16
PACK_VMEM = 24
NT = (((1,), (1,)), ((), ()))
NN = (((1,), (0,)), ((), ()))
TN = (((0,), (0,)), ((), ()))
VM = pl.BlockSpec(memory_space=pltpu.VMEM)
SM = pl.BlockSpec(memory_space=pltpu.SMEM)


def send(x, to, back=False):
    perm = []
    for z in range(ZS):
        for xh in range(2):
            for c in range(2):
                tz, tx, tc = to(z, xh, c)
                perm.append((z * 4 + xh * 2 + c, (tz % ZS) * 4 + tx * 2 + tc))
    return lax.ppermute(x, "ctx", [(b, a) for a, b in perm] if back else perm)


def core(z, xh, c):
    return z, xh, 1 - c


def ring(z, xh, c):
    return z + 1 - 2 * c, xh, c


def chip(z, xh, c):
    return z, 1 - xh, c ^ xh


def ring2(z, xh, c):
    return z + 2 * (1 - 2 * c), xh, c


def split(x):
    hi = x.astype(BF16)
    return hi, (x - hi.astype(F32)).astype(BF16)


def dot(a, b, dims=NN):
    return lax.dot_general(a, b, dims, preferred_element_type=F32)


def pack_kernel(rank_ref, order_ref, q_hbm, do_hbm, o_hbm, lse_hbm, p_ref, a_ref, b_ref, q, do, o, lse_ref, sems):
    copies = [
        pltpu.make_async_copy(do_hbm, do, sems.at[0]),
        pltpu.make_async_copy(o_hbm, o, sems.at[1]),
        pltpu.make_async_copy(q_hbm, q, sems.at[2]),
        pltpu.make_async_copy(lse_hbm, lse_ref, sems.at[3]),
    ]
    for copy in copies:
        copy.start()
    rows = q.shape[0]
    lane = lax.broadcasted_iota(jnp.int32, (rows, DH), 1)
    row = lax.broadcasted_iota(jnp.int32, (rows, DH), 0)
    slot = rank_ref[0] * 2
    pos = jnp.where(row < HALF, order_ref[slot], order_ref[slot + 1])
    x = jnp.where((lane < HALF) & (lane > pos), -BIG, 0.0)

    def put(into, column, first):
        hi = column.astype(BF16).astype(F32)
        mid = (column - hi).astype(BF16).astype(F32)
        lo = column - hi - mid
        at = lane - first
        return jnp.where(at == 0, hi, jnp.where(at == 1, mid, jnp.where(at == 2, lo, into)))

    copies[3].wait()
    lse = jnp.concatenate([lse_ref[...] * (-LOG2E), jnp.zeros((DH - HQ, rows), F32)], axis=0).T
    for h in range(HQ):
        x = put(x, jnp.sum(jnp.where(lane == h, lse, 0.0), axis=1, keepdims=True), HALF + 3 * h)
    copies[0].wait()
    copies[1].wait()
    for h in range(HQ):
        s = slice(h * DH, (h + 1) * DH)
        x = put(x, -jnp.sum(do[:, s] * o[:, s], axis=1, keepdims=True), HALF + 3 * (HQ + h))
    w = CHUNK * DH
    p_ref[:, 2 * w : 4 * w] = do[...]
    a_ref[:, w : 2 * w] = do[:, :w]
    b_ref[:, w:] = do[:, w:]
    p_ref[:, 4 * w :] = x
    a_ref[:, 2 * w :] = x
    copies[2].wait()
    scaled = q[...] * (LOG2E / math.sqrt(DH))
    p_ref[:, : 2 * w] = scaled
    a_ref[:, :w] = scaled[:, :w]
    b_ref[:, :w] = scaled[:, w:]


def pack(rank, order, query, grad_output, output, lse):
    rows = query.shape[0]
    hbm = pl.BlockSpec(memory_space=pltpu.HBM)
    return pl.pallas_call(
        pack_kernel,
        in_specs=[SM, SM, hbm, hbm, hbm, hbm],
        out_specs=[VM] * 3,
        out_shape=[jax.ShapeDtypeStruct((rows, n * DH), F32) for n in (2 * HQ + 1, HQ + 1, HQ)],
        scratch_shapes=[pltpu.VMEM((rows, HQ * DH), F32)] * 3
        + [pltpu.VMEM((HQ, rows), F32), pltpu.SemaphoreType.DMA((4,))],
        compiler_params=pltpu.CompilerParams(vmem_limit_bytes=PACK_VMEM * 2**20),
        cost_estimate=pl.CostEstimate(flops=2**32, bytes_accessed=2**21, transcendentals=0),
        name="pack",
    )(rank, *[pltpu.with_memory_space_constraint(x, pltpu.HBM) for x in (order, query, grad_output, output, lse)])


def half_kernel(rank_ref, b_ref, out_ref):
    first = pl.multiple_of((rank_ref[0] % 2) * HALF, HALF)
    out_ref[:HALF] = b_ref[pl.ds(first, HALF)]
    out_ref[HALF:] = b_ref[pl.ds(first + 2 * HALF, HALF)]


def join_kernel(rank_ref, r_ref, b_ref, r4_ref, out_ref):
    first = pl.multiple_of((rank_ref[0] % 2) * HALF, HALF)
    out_ref[...] = r_ref[...] + b_ref[...]
    out_ref[pl.ds(first, HALF)] += r4_ref[:HALF]
    out_ref[pl.ds(first + 2 * HALF, HALF)] += r4_ref[HALF:]


def part_kernel(rank_ref, r_ref, later_ref, mine_ref, other_ref):
    mine_ref[...] = r_ref[: 2 * HALF]
    other_ref[...] = r_ref[2 * HALF :]


def small(kernel, n, lines, *args):
    shape = jax.ShapeDtypeStruct((2 * HALF * lines, 2 * DH), F32)
    return pl.pallas_call(
        kernel,
        in_specs=[SM] + [VM if a.shape[1] == 2 * DH else pl.BlockSpec(memory_space=pl.ANY) for a in args[1:]],
        out_specs=[VM] * n,
        out_shape=[shape] * n,
        compiler_params=pltpu.CompilerParams(vmem_limit_bytes=4 * 2**20),
        name=kernel.__name__,
    )(*args)


def tie_kernel(x_ref, sign_ref, out_ref):
    pass


def names_of(jobs):
    names = []
    for gs, halves in jobs:
        for g in gs:
            names += [(g, None)] if g in ("self", "core") else [(g, half) for half in (0, *halves)]
    return list(dict.fromkeys(names))


def grads_kernel(steps, jobs, dq_from, dq_old, has_dkv, ties, *refs):
    refs = list(refs)
    take = lambda n: [refs.pop(0) for _ in range(n)]
    rank_ref, order_ref = take(2)
    groups = list(dict.fromkeys(g for gs, _ in jobs for g in gs))
    names = names_of(jobs)
    packs = dict(zip(names, take(len(names))))
    kv_refs = take(len(steps))
    dq_in = dict(zip(dq_from, take(len(dq_from))))
    dkv_in = dict(zip(has_dkv, take(len(has_dkv))))
    take(ties)
    dq_out = dict(zip(groups, take(len(groups))))
    dkv_out = take(len(steps))
    sign = refs.pop(0)
    sign[...] = jnp.zeros_like(sign)
    kc, vc = take(2)

    rank = rank_ref[0]
    z, xh, c = rank // 4, (rank // 2) % 2, rank % 2
    lane = lax.broadcasted_iota(jnp.int32, (HALF, DH), 1)
    at = 0
    for step, ref in zip(steps, kv_refs):
        zk = lax.rem(z + (2 * c - 1) * step + ZS, ZS)
        for i in range(ref.shape[0] // HALF):
            if step < ZS // 2:
                line, part = (c if i < 2 else 1 - c), i % 2
            else:
                line, part = (c if i < 1 else 1 - c), c
            pos = order_ref[(zk * 4 + xh * 2 + line) * 2 + part]
            hot = jnp.where((lane == pos) | (lane >= HALF), 1.0, 0.0).astype(BF16)
            s, to = slice(i * HALF, (i + 1) * HALF), slice(at, at + HALF)
            hi, lo = split(ref[s, :DH])
            kc[to, :] = jnp.concatenate([hi, lo, hi, hot], axis=1)
            hi, lo = split(ref[s, DH:])
            vc[to, :] = jnp.concatenate([hi, lo, hi, hot], axis=1)
            at += HALF

    lane = lax.broadcasted_iota(jnp.int32, (DH, DH), 1)
    first = True
    for gs, half in ((gs, half) for gs, halves in jobs for half in halves):
        qs, ds = [], []
        for h in range(CHUNK):
            head = half * CHUNK + h
            mine = (lane < HALF) | ((lane - HALF) // 3 == head)
            mine_do = (lane - HALF) // 3 == HQ + head
            for g in gs:
                if (g, None) in packs:
                    ref, q_at, do_at = packs[g, None], head * DH, (HQ + head) * DH
                    terms = ref[:, 2 * HQ * DH :]
                else:
                    ref, q_at, do_at = packs[g, half], h * DH, (CHUNK + h) * DH
                    terms = packs[g, 0][:, 2 * CHUNK * DH :]
                hi, lo = split(ref[:, q_at : q_at + DH])
                bias = jnp.where(mine, terms, 0.0).astype(BF16)
                qs.append(jnp.concatenate([hi, hi, lo, bias], axis=1))
                hi, lo = split(ref[:, do_at : do_at + DH])
                bias = jnp.where(mine_do, terms, 0.0).astype(BF16)
                ds.append(jnp.concatenate([hi, hi, lo, bias], axis=1))
        qc, dc = jnp.concatenate(qs, axis=0), jnp.concatenate(ds, axis=0)
        p = jnp.exp2(dot(kc[...], qc, NT))
        if 0 in steps and "self" in gs:
            top = p[:DH]
            a = lax.broadcasted_iota(jnp.int32, top.shape, 0)
            b = lax.broadcasted_iota(jnp.int32, top.shape, 1)
            rows = len(gs) * DH
            b = b - (b // rows) * rows - gs.index("self") * DH
            top = jnp.where((b >= 0) & (b < DH) & (a // HALF == b // HALF) & (a > b), 0.0, top)
            p = top if p.shape[0] == DH else jnp.concatenate([top, p[DH:]], axis=0)
        d = p * dot(vc[...], dc, NT)
        p_hi, p_lo = split(p)
        r = dot(p_hi, dc[:, DH : 3 * DH])
        dv = r[:, :DH] + r[:, DH:] + dot(p_lo, dc[:, :DH])
        d_hi, d_lo = split(d)
        r = dot(d_hi, qc[:, DH : 3 * DH])
        dk = (r[:, :DH] + r[:, DH:] + dot(d_lo, qc[:, :DH])) * (1.0 / LOG2E)
        at = 0
        for step, out in zip(steps, dkv_out):
            s = slice(at, at + out.shape[0])
            at += out.shape[0]
            if first:
                out[:, :DH] = dkv_in[step][:, :DH] + dk[s] if step in dkv_in else dk[s]
                out[:, DH:] = dkv_in[step][:, DH:] + dv[s] if step in dkv_in else dv[s]
            else:
                out[:, :DH] += dk[s]
                out[:, DH:] += dv[s]
        first = False
        r = dot(d_hi, kc[:, : 2 * DH], TN)
        dq = (r[:, :DH] + r[:, DH:] + dot(d_lo, kc[:, :DH], TN)) * (1.0 / math.sqrt(DH))
        for h in range(CHUNK):
            for j, g in enumerate(gs):
                s = slice((half * CHUNK + h) * DH, (half * CHUNK + h + 1) * DH)
                t = dq[(h * len(gs) + j) * DH : (h * len(gs) + j + 1) * DH]
                dq_out[g][:, s] = dq_in[g][:, s] + t if (g, half) in dq_old else t


class Totals:
    def __init__(self, rank, order, packs, blocks):
        self.rank, self.order, self.packs, self.blocks = rank, order, packs, blocks
        self.dq, self.held, self.dkv, self.last = {}, set(), {}, None

    def after(self, x):
        any_ = pl.BlockSpec(memory_space=pl.ANY)
        return pl.pallas_call(
            tie_kernel,
            in_specs=[any_, any_],
            out_specs=any_,
            out_shape=jax.ShapeDtypeStruct(x.shape, x.dtype),
            input_output_aliases={0: 0},
            compiler_params=pltpu.CompilerParams(vmem_limit_bytes=2**20),
            name="tie",
        )(x, self.last)

    def add(self, steps, *jobs, need=(), flops=2**10):
        groups = list(dict.fromkeys(g for gs, _ in jobs for g in gs))
        args = [self.packs[n] for n in names_of(jobs)] + [self.blocks[s] for s in steps]
        dq_from = [g for g in groups if g in self.dq]
        dq_old = frozenset(self.held)
        self.held.update((g, half) for gs, halves in jobs for g in gs for half in halves)
        has_dkv = [s for s in steps if s in self.dkv]
        aliases = {}
        for g in dq_from:
            aliases[2 + len(args)] = groups.index(g)
            args.append(self.dq[g])
        for s in has_dkv:
            aliases[2 + len(args)] = len(groups) + steps.index(s)
            args.append(self.dkv[s])
        ties = [*need] if self.last is None else [self.last, *need]
        args += ties
        rows = [self.blocks[s].shape[0] for s in steps]
        keys = sum(rows)
        outs = pl.pallas_call(
            functools.partial(grads_kernel, steps, jobs, dq_from, dq_old, has_dkv, len(ties)),
            in_specs=[SM, SM] + [VM] * (len(args) - len(ties)) + [pl.BlockSpec(memory_space=pl.ANY)] * len(ties),
            out_specs=[VM] * (len(groups) + len(steps) + 1),
            out_shape=[jax.ShapeDtypeStruct((DH, HQ * DH), F32)] * len(groups)
            + [jax.ShapeDtypeStruct((n, 2 * DH), F32) for n in rows]
            + [jax.ShapeDtypeStruct((8, DH), F32)],
            input_output_aliases=aliases,
            scratch_shapes=[pltpu.VMEM((keys, 4 * DH), BF16)] * 2,
            compiler_params=pltpu.CompilerParams(vmem_limit_bytes=(8 + keys // 40) * 2**20),
            cost_estimate=pl.CostEstimate(flops=flops, bytes_accessed=2**10, transcendentals=0),
            name="grads_" + "".join(map(str, steps)) + "_" + "_".join(gs[0] + "ab"[halves[0] : halves[-1] + 1] for gs, halves in jobs),
        )(self.rank, self.order, *args)
        self.dq.update(zip(groups, outs))
        self.dkv.update(zip(steps, outs[len(groups) : -1]))
        self.last = outs[-1]


def local(query, key, value, output, grad_output, lse, span_order):
    rank = lax.axis_index("ctx").astype(jnp.int32).reshape(1)
    c = rank[0] % 2
    kv = jnp.concatenate([key, value], axis=1)
    kv_c = send(kv, core)
    p, pa, pb = pack(rank, span_order, query, grad_output, output, lse)
    packs = {("self", None): p, ("x", 0): send(pa, chip), ("core", None): send(p, core)}
    blocks = {0: kv}
    total = Totals(rank, span_order, packs, blocks)
    after = total.after
    own, other = ("self", "core"), ("x", "v")
    both = (0, 1)
    blocks[1] = send(jnp.concatenate([kv, kv_c], axis=0), ring)
    total.add([0], (own, both))
    blocks[1] = after(blocks[1])
    blocks[2] = send(blocks[1], ring)
    total.add([1], (own, both))
    packs["x", 0] = after(packs["x", 0])
    packs["v", 0] = send(packs["x", 0], core)
    packs["x", 1] = send(after(pb), chip)
    blocks[2] = after(blocks[2])
    blocks[3] = send(blocks[2], ring)
    total.add([2], (own, both), flops=2**37)
    total.add([0, 1, 2], (other, (0,)))
    blocks[3] = after(blocks[3])
    blocks[4] = send(small(half_kernel, 1, 1, rank, blocks[3])[0], ring)
    total.add([3], (own, both))
    packs["x", 1] = after(packs["x", 1])
    packs["v", 1] = send(packs["x", 1], core)
    total.add([3], (other, (0,)), need=[blocks[4]], flops=2**37)
    total.add([3], (other, (1,)))
    r = send(total.dkv[3], ring, back=True)
    total.add([4], (other, both), (own, both), flops=2**37)
    total.add([0, 1, 2], (other, (1,)), need=[r])
    r4 = send(total.dkv[4], ring2, back=True)
    r = send(small(join_kernel, 1, 2, rank, r, total.dkv[2], r4)[0], ring, back=True)
    w = 2 * DH
    dq_v = jnp.concatenate([send(total.dq["v"][:, i : i + w], core) for i in range(0, HQ * DH, w)], axis=1)
    dq_x = send(total.dq["x"] + dq_v, chip, back=True)
    r = send(total.dkv[1] + r, ring, back=True)
    r, r_c = small(part_kernel, 2, 1, rank, r, dq_x)
    dkv = total.dkv[0] + r + send(r_c, core)
    dq = total.dq["self"] + send(total.dq["core"], core) + dq_x
    return dq, dkv[:, :DH], dkv[:, DH:]


def solution(mesh):
    in_specs = (
        P("ctx", "heads"),
        P("ctx", "heads"),
        P("ctx", "heads"),
        P("ctx", "heads"),
        P("ctx", "heads"),
        P("heads", "ctx"),
        P("heads"),
    )
    out_specs = (P("ctx", "heads"), P("ctx", "heads"), P("ctx", "heads"))
    return jax.shard_map(local, mesh=mesh, in_specs=in_specs, out_specs=out_specs, check_vma=False)
```

```python
import functools
import math

import jax
import jax.numpy as jnp
from jax import lax
from jax.experimental import pallas as pl
from jax.experimental.pallas import tpu as pltpu
from jax.sharding import PartitionSpec as P

ZS = 8
DH = 128
HQ = 8
CHUNK = 4
HALF = 64
LOG2E = 1.4426950408889634
BIG = 1e30
F32 = jnp.float32
BF16 = jnp.bfloat16
PACK_VMEM = 24
NT = (((1,), (1,)), ((), ()))
NN = (((1,), (0,)), ((), ()))
TN = (((0,), (0,)), ((), ()))
VM = pl.BlockSpec(memory_space=pltpu.VMEM)
SM = pl.BlockSpec(memory_space=pltpu.SMEM)


def send(x, to, back=False):
    perm = []
    for z in range(ZS):
        for xh in range(2):
            for c in range(2):
                tz, tx, tc = to(z, xh, c)
                perm.append((z * 4 + xh * 2 + c, (tz % ZS) * 4 + tx * 2 + tc))
    return lax.ppermute(x, "ctx", [(b, a) for a, b in perm] if back else perm)


def core(z, xh, c):
    return z, xh, 1 - c


def ring(z, xh, c):
    return z + 1 - 2 * c, xh, c


def chip(z, xh, c):
    return z, 1 - xh, c ^ xh


def across(z, xh, c):
    return z + ZS // 2, xh, c


def split(x):
    hi = x.astype(BF16)
    return hi, (x - hi.astype(F32)).astype(BF16)


def dot(a, b, dims=NN):
    return lax.dot_general(a, b, dims, preferred_element_type=F32)


def pack_kernel(rank_ref, order_ref, q_hbm, do_hbm, o_hbm, lse_hbm, p_ref, a_ref, b_ref, q, do, o, lse_ref, sems):
    copies = [
        pltpu.make_async_copy(do_hbm, do, sems.at[0]),
        pltpu.make_async_copy(o_hbm, o, sems.at[1]),
        pltpu.make_async_copy(q_hbm, q, sems.at[2]),
        pltpu.make_async_copy(lse_hbm, lse_ref, sems.at[3]),
    ]
    for copy in copies:
        copy.start()
    rows = q.shape[0]
    lane = lax.broadcasted_iota(jnp.int32, (rows, DH), 1)
    row = lax.broadcasted_iota(jnp.int32, (rows, DH), 0)
    slot = rank_ref[0] * 2
    pos = jnp.where(row < HALF, order_ref[slot], order_ref[slot + 1])
    x = jnp.where((lane < HALF) & (lane > pos), -BIG, 0.0)

    def put(into, column, first):
        hi = column.astype(BF16).astype(F32)
        mid = (column - hi).astype(BF16).astype(F32)
        lo = column - hi - mid
        at = lane - first
        return jnp.where(at == 0, hi, jnp.where(at == 1, mid, jnp.where(at == 2, lo, into)))

    copies[3].wait()
    lse = jnp.concatenate([lse_ref[...] * (-LOG2E), jnp.zeros((DH - HQ, rows), F32)], axis=0).T
    for h in range(HQ):
        x = put(x, jnp.sum(jnp.where(lane == h, lse, 0.0), axis=1, keepdims=True), HALF + 3 * h)
    copies[0].wait()
    copies[1].wait()
    for h in range(HQ):
        s = slice(h * DH, (h + 1) * DH)
        x = put(x, -jnp.sum(do[:, s] * o[:, s], axis=1, keepdims=True), HALF + 3 * (HQ + h))
    w = CHUNK * DH
    p_ref[:, 2 * w : 4 * w] = do[...]
    a_ref[:, w : 2 * w] = do[:, :w]
    b_ref[:, w:] = do[:, w:]
    p_ref[:, 4 * w :] = x
    a_ref[:, 2 * w :] = x
    copies[2].wait()
    scaled = q[...] * (LOG2E / math.sqrt(DH))
    p_ref[:, : 2 * w] = scaled
    a_ref[:, :w] = scaled[:, :w]
    b_ref[:, :w] = scaled[:, w:]


def pack(rank, order, query, grad_output, output, lse):
    rows = query.shape[0]
    hbm = pl.BlockSpec(memory_space=pltpu.HBM)
    return pl.pallas_call(
        pack_kernel,
        in_specs=[SM, SM, hbm, hbm, hbm, hbm],
        out_specs=[VM] * 3,
        out_shape=[jax.ShapeDtypeStruct((rows, n * DH), F32) for n in (2 * HQ + 1, HQ + 1, HQ)],
        scratch_shapes=[pltpu.VMEM((rows, HQ * DH), F32)] * 3
        + [pltpu.VMEM((HQ, rows), F32), pltpu.SemaphoreType.DMA((4,))],
        compiler_params=pltpu.CompilerParams(vmem_limit_bytes=PACK_VMEM * 2**20),
        cost_estimate=pl.CostEstimate(flops=2**32, bytes_accessed=2**21, transcendentals=0),
        name="pack",
    )(rank, *[pltpu.with_memory_space_constraint(x, pltpu.HBM) for x in (order, query, grad_output, output, lse)])


def half_kernel(rank_ref, b_ref, out_ref):
    first = pl.multiple_of((rank_ref[0] % 2) * HALF, HALF)
    out_ref[:HALF] = b_ref[pl.ds(first, HALF)]
    out_ref[HALF:] = b_ref[pl.ds(first + 2 * HALF, HALF)]


def line_kernel(rank_ref, b_ref, got_ref, out_ref):
    first = pl.multiple_of((rank_ref[0] % 2) * HALF, HALF)
    out_ref[pl.ds(first, HALF)] = b_ref[:HALF]
    out_ref[pl.ds(HALF - first, HALF)] = got_ref[...]


def part_kernel(rank_ref, r_ref, later_ref, mine_ref, other_ref):
    mine_ref[...] = r_ref[: 2 * HALF]
    other_ref[...] = r_ref[2 * HALF :]


def small(kernel, n, *args):
    shape = jax.ShapeDtypeStruct((2 * HALF, 2 * DH), F32)
    return pl.pallas_call(
        kernel,
        in_specs=[SM] + [VM if a.shape[1] == 2 * DH else pl.BlockSpec(memory_space=pl.ANY) for a in args[1:]],
        out_specs=[VM] * n,
        out_shape=[shape] * n,
        compiler_params=pltpu.CompilerParams(vmem_limit_bytes=4 * 2**20),
        name=kernel.__name__,
    )(*args)


def tie_kernel(x_ref, sign_ref, out_ref):
    pass


def names_of(jobs):
    names = []
    for gs, halves in jobs:
        for g in gs:
            names += [(g, None)] if g in ("self", "core") else [(g, half) for half in (0, *halves)]
    return list(dict.fromkeys(names))


def grads_kernel(steps, jobs, dq_from, dq_old, has_dkv, ties, *refs):
    refs = list(refs)
    take = lambda n: [refs.pop(0) for _ in range(n)]
    rank_ref, order_ref = take(2)
    groups = list(dict.fromkeys(g for gs, _ in jobs for g in gs))
    names = names_of(jobs)
    packs = dict(zip(names, take(len(names))))
    kv_refs = take(len(steps))
    dq_in = dict(zip(dq_from, take(len(dq_from))))
    dkv_in = dict(zip(has_dkv, take(len(has_dkv))))
    take(ties)
    dq_out = dict(zip(groups, take(len(groups))))
    dkv_out = take(len(steps))
    sign = refs.pop(0)
    sign[...] = jnp.zeros_like(sign)
    kc, vc = take(2)

    rank = rank_ref[0]
    z, xh, c = rank // 4, (rank // 2) % 2, rank % 2
    lane = lax.broadcasted_iota(jnp.int32, (HALF, DH), 1)
    at = 0
    for step, ref in zip(steps, kv_refs):
        zk = lax.rem(z + (2 * c - 1) * step + ZS, ZS)
        for i in range(ref.shape[0] // HALF):
            if step < ZS // 2:
                line, part = (c if i < 2 else 1 - c), i % 2
            else:
                line, part = (c if i < 1 else 1 - c), c
            pos = order_ref[(zk * 4 + xh * 2 + line) * 2 + part]
            hot = jnp.where((lane == pos) | (lane >= HALF), 1.0, 0.0).astype(BF16)
            s, to = slice(i * HALF, (i + 1) * HALF), slice(at, at + HALF)
            hi, lo = split(ref[s, :DH])
            kc[to, :] = jnp.concatenate([hi, lo, hi, hot], axis=1)
            hi, lo = split(ref[s, DH:])
            vc[to, :] = jnp.concatenate([hi, lo, hi, hot], axis=1)
            at += HALF

    lane = lax.broadcasted_iota(jnp.int32, (DH, DH), 1)
    first = True
    for gs, half in ((gs, half) for gs, halves in jobs for half in halves):
        qs, ds = [], []
        for h in range(CHUNK):
            head = half * CHUNK + h
            mine = (lane < HALF) | ((lane - HALF) // 3 == head)
            mine_do = (lane - HALF) // 3 == HQ + head
            for g in gs:
                if (g, None) in packs:
                    ref, q_at, do_at = packs[g, None], head * DH, (HQ + head) * DH
                    terms = ref[:, 2 * HQ * DH :]
                else:
                    ref, q_at, do_at = packs[g, half], h * DH, (CHUNK + h) * DH
                    terms = packs[g, 0][:, 2 * CHUNK * DH :]
                hi, lo = split(ref[:, q_at : q_at + DH])
                bias = jnp.where(mine, terms, 0.0).astype(BF16)
                qs.append(jnp.concatenate([hi, hi, lo, bias], axis=1))
                hi, lo = split(ref[:, do_at : do_at + DH])
                bias = jnp.where(mine_do, terms, 0.0).astype(BF16)
                ds.append(jnp.concatenate([hi, hi, lo, bias], axis=1))
        qc, dc = jnp.concatenate(qs, axis=0), jnp.concatenate(ds, axis=0)
        p = jnp.exp2(dot(kc[...], qc, NT))
        if 0 in steps and "self" in gs:
            top = p[:DH]
            a = lax.broadcasted_iota(jnp.int32, top.shape, 0)
            b = lax.broadcasted_iota(jnp.int32, top.shape, 1)
            rows = len(gs) * DH
            b = b - (b // rows) * rows - gs.index("self") * DH
            top = jnp.where((b >= 0) & (b < DH) & (a // HALF == b // HALF) & (a > b), 0.0, top)
            p = top if p.shape[0] == DH else jnp.concatenate([top, p[DH:]], axis=0)
        d = p * dot(vc[...], dc, NT)
        p_hi, p_lo = split(p)
        r = dot(p_hi, dc[:, DH : 3 * DH])
        dv = r[:, :DH] + r[:, DH:] + dot(p_lo, dc[:, :DH])
        d_hi, d_lo = split(d)
        r = dot(d_hi, qc[:, DH : 3 * DH])
        dk = (r[:, :DH] + r[:, DH:] + dot(d_lo, qc[:, :DH])) * (1.0 / LOG2E)
        at = 0
        for step, out in zip(steps, dkv_out):
            s = slice(at, at + out.shape[0])
            at += out.shape[0]
            if first:
                out[:, :DH] = dkv_in[step][:, :DH] + dk[s] if step in dkv_in else dk[s]
                out[:, DH:] = dkv_in[step][:, DH:] + dv[s] if step in dkv_in else dv[s]
            else:
                out[:, :DH] += dk[s]
                out[:, DH:] += dv[s]
        first = False
        r = dot(d_hi, kc[:, : 2 * DH], TN)
        dq = (r[:, :DH] + r[:, DH:] + dot(d_lo, kc[:, :DH], TN)) * (1.0 / math.sqrt(DH))
        for h in range(CHUNK):
            for j, g in enumerate(gs):
                s = slice((half * CHUNK + h) * DH, (half * CHUNK + h + 1) * DH)
                t = dq[(h * len(gs) + j) * DH : (h * len(gs) + j + 1) * DH]
                dq_out[g][:, s] = dq_in[g][:, s] + t if (g, half) in dq_old else t


class Totals:
    def __init__(self, rank, order, packs, blocks):
        self.rank, self.order, self.packs, self.blocks = rank, order, packs, blocks
        self.dq, self.held, self.dkv, self.last = {}, set(), {}, None

    def after(self, x):
        any_ = pl.BlockSpec(memory_space=pl.ANY)
        return pl.pallas_call(
            tie_kernel,
            in_specs=[any_, any_],
            out_specs=any_,
            out_shape=jax.ShapeDtypeStruct(x.shape, x.dtype),
            input_output_aliases={0: 0},
            compiler_params=pltpu.CompilerParams(vmem_limit_bytes=2**20),
            name="tie",
        )(x, self.last)

    def add(self, steps, *jobs, need=(), flops=2**10):
        groups = list(dict.fromkeys(g for gs, _ in jobs for g in gs))
        args = [self.packs[n] for n in names_of(jobs)] + [self.blocks[s] for s in steps]
        dq_from = [g for g in groups if g in self.dq]
        dq_old = frozenset(self.held)
        self.held.update((g, half) for gs, halves in jobs for g in gs for half in halves)
        has_dkv = [s for s in steps if s in self.dkv]
        aliases = {}
        for g in dq_from:
            aliases[2 + len(args)] = groups.index(g)
            args.append(self.dq[g])
        for s in has_dkv:
            aliases[2 + len(args)] = len(groups) + steps.index(s)
            args.append(self.dkv[s])
        ties = [*need] if self.last is None else [self.last, *need]
        args += ties
        rows = [self.blocks[s].shape[0] for s in steps]
        keys = sum(rows)
        outs = pl.pallas_call(
            functools.partial(grads_kernel, steps, jobs, dq_from, dq_old, has_dkv, len(ties)),
            in_specs=[SM, SM] + [VM] * (len(args) - len(ties)) + [pl.BlockSpec(memory_space=pl.ANY)] * len(ties),
            out_specs=[VM] * (len(groups) + len(steps) + 1),
            out_shape=[jax.ShapeDtypeStruct((DH, HQ * DH), F32)] * len(groups)
            + [jax.ShapeDtypeStruct((n, 2 * DH), F32) for n in rows]
            + [jax.ShapeDtypeStruct((8, DH), F32)],
            input_output_aliases=aliases,
            scratch_shapes=[pltpu.VMEM((keys, 4 * DH), BF16)] * 2,
            compiler_params=pltpu.CompilerParams(vmem_limit_bytes=(8 + keys // 40) * 2**20),
            cost_estimate=pl.CostEstimate(flops=flops, bytes_accessed=2**10, transcendentals=0),
            name="grads_" + "".join(map(str, steps)) + "_" + "_".join(gs[0] + "ab"[halves[0] : halves[-1] + 1] for gs, halves in jobs),
        )(self.rank, self.order, *args)
        self.dq.update(zip(groups, outs))
        self.dkv.update(zip(steps, outs[len(groups) : -1]))
        self.last = outs[-1]


def local(query, key, value, output, grad_output, lse, span_order):
    rank = lax.axis_index("ctx").astype(jnp.int32).reshape(1)
    c = rank[0] % 2
    kv = jnp.concatenate([key, value], axis=1)
    kv_c = send(kv, core)
    p, pa, pb = pack(rank, span_order, query, grad_output, output, lse)
    packs = {("self", None): p, ("x", 0): send(pa, chip), ("core", None): send(p, core)}
    blocks = {0: kv}
    total = Totals(rank, span_order, packs, blocks)
    after = total.after
    own, other = ("self", "core"), ("x", "v")
    both = (0, 1)
    blocks[1] = send(jnp.concatenate([kv, kv_c], axis=0), ring)
    total.add([0], (own, both))
    blocks[1] = after(blocks[1])
    blocks[2] = send(blocks[1], ring)
    total.add([1], (own, both))
    packs["x", 0] = after(packs["x", 0])
    packs["v", 0] = send(packs["x", 0], core)
    packs["x", 1] = send(after(pb), chip)
    blocks[2] = after(blocks[2])
    blocks[3] = send(blocks[2], ring)
    total.add([2], (own, both), flops=2**37)
    total.add([0, 1, 2], (other, (0,)))
    blocks[3] = after(blocks[3])
    blocks[4] = send(small(half_kernel, 1, rank, blocks[3])[0], ring)
    total.add([3], (own, both))
    packs["x", 1] = after(packs["x", 1])
    packs["v", 1] = send(packs["x", 1], core)
    total.add([3], (other, (0,)), need=[blocks[4]], flops=2**37)
    total.add([3], (other, (1,)))
    r = send(total.dkv[3], ring, back=True)
    total.add([4], (other, both), (own, both), flops=2**37)
    total.add([0, 1, 2], (other, (1,)), need=[r])
    r = send(total.dkv[2] + r, ring, back=True)
    dq_x = total.dq["x"] + send(total.dq["v"], core)
    dq_x = send(dq_x, chip, back=True)
    r4 = small(line_kernel, 1, rank, total.dkv[4], send(total.dkv[4][HALF:], core))[0]
    total.last = r4
    r = after(total.dkv[1] + r)
    r4 = send(jnp.pad(r4, ((0, 8), (0, 0))), across)[: 2 * HALF]
    r = send(r, ring, back=True)
    r, r_c = small(part_kernel, 2, rank, r, dq_x)
    dkv = total.dkv[0] + r + send(r_c, core) + r4
    dq = total.dq["self"] + send(total.dq["core"], core) + dq_x
    return dq, dkv[:, :DH], dkv[:, DH:]


def solution(mesh):
    in_specs = (
        P("ctx", "heads"),
        P("ctx", "heads"),
        P("ctx", "heads"),
        P("ctx", "heads"),
        P("ctx", "heads"),
        P("heads", "ctx"),
        P("heads"),
    )
    out_specs = (P("ctx", "heads"), P("ctx", "heads"), P("ctx", "heads"))
    return jax.shard_map(local, mesh=mesh, in_specs=in_specs, out_specs=out_specs, check_vma=False)
```

```python
import functools
import math

import jax
import jax.numpy as jnp
from jax import lax
from jax.experimental import pallas as pl
from jax.experimental.pallas import tpu as pltpu
from jax.sharding import PartitionSpec as P

ZS = 8
DH = 128
HQ = 8
CHUNK = 4
HALF = 64
LOG2E = 1.4426950408889634
BIG = 1e30
F32 = jnp.float32
BF16 = jnp.bfloat16
PACK_VMEM = 24
NT = (((1,), (1,)), ((), ()))
NN = (((1,), (0,)), ((), ()))
TN = (((0,), (0,)), ((), ()))
VM = pl.BlockSpec(memory_space=pltpu.VMEM)
SM = pl.BlockSpec(memory_space=pltpu.SMEM)


def send(x, to, back=False):
    perm = []
    for z in range(ZS):
        for xh in range(2):
            for c in range(2):
                tz, tx, tc = to(z, xh, c)
                perm.append((z * 4 + xh * 2 + c, (tz % ZS) * 4 + tx * 2 + tc))
    return lax.ppermute(x, "ctx", [(b, a) for a, b in perm] if back else perm)


def core(z, xh, c):
    return z, xh, 1 - c


def ring(z, xh, c):
    return z + 1 - 2 * c, xh, c


def chip(z, xh, c):
    return z, 1 - xh, c


def across(z, xh, c):
    return z + ZS // 2, xh, c


def split(x):
    hi = x.astype(BF16)
    return hi, (x - hi.astype(F32)).astype(BF16)


def dot(a, b, dims=NN):
    return lax.dot_general(a, b, dims, preferred_element_type=F32)


def pack_kernel(rank_ref, order_ref, q_hbm, do_hbm, o_hbm, lse_hbm, p_ref, a_ref, b_ref, q, do, o, lse_ref, sems):
    copies = [
        pltpu.make_async_copy(do_hbm, do, sems.at[0]),
        pltpu.make_async_copy(o_hbm, o, sems.at[1]),
        pltpu.make_async_copy(q_hbm, q, sems.at[2]),
        pltpu.make_async_copy(lse_hbm, lse_ref, sems.at[3]),
    ]
    for copy in copies:
        copy.start()
    rows = q.shape[0]
    lane = lax.broadcasted_iota(jnp.int32, (rows, DH), 1)
    row = lax.broadcasted_iota(jnp.int32, (rows, DH), 0)
    slot = rank_ref[0] * 2
    pos = jnp.where(row < HALF, order_ref[slot], order_ref[slot + 1])
    x = jnp.where((lane < HALF) & (lane > pos), -BIG, 0.0)

    def put(into, column, first):
        hi = column.astype(BF16).astype(F32)
        mid = (column - hi).astype(BF16).astype(F32)
        lo = column - hi - mid
        at = lane - first
        return jnp.where(at == 0, hi, jnp.where(at == 1, mid, jnp.where(at == 2, lo, into)))

    copies[3].wait()
    lse = jnp.concatenate([lse_ref[...] * (-LOG2E), jnp.zeros((DH - HQ, rows), F32)], axis=0).T
    for h in range(HQ):
        x = put(x, jnp.sum(jnp.where(lane == h, lse, 0.0), axis=1, keepdims=True), HALF + 3 * h)
    copies[0].wait()
    copies[1].wait()
    for h in range(HQ):
        s = slice(h * DH, (h + 1) * DH)
        x = put(x, -jnp.sum(do[:, s] * o[:, s], axis=1, keepdims=True), HALF + 3 * (HQ + h))
    w = CHUNK * DH
    p_ref[:, 2 * w : 4 * w] = do[...]
    a_ref[:, w : 2 * w] = do[:, :w]
    b_ref[:, w:] = do[:, w:]
    p_ref[:, 4 * w :] = x
    a_ref[:, 2 * w :] = x
    copies[2].wait()
    scaled = q[...] * (LOG2E / math.sqrt(DH))
    p_ref[:, : 2 * w] = scaled
    a_ref[:, :w] = scaled[:, :w]
    b_ref[:, :w] = scaled[:, w:]


def pack(rank, order, query, grad_output, output, lse):
    rows = query.shape[0]
    hbm = pl.BlockSpec(memory_space=pltpu.HBM)
    return pl.pallas_call(
        pack_kernel,
        in_specs=[SM, SM, hbm, hbm, hbm, hbm],
        out_specs=[VM] * 3,
        out_shape=[jax.ShapeDtypeStruct((rows, n * DH), F32) for n in (2 * HQ + 1, HQ + 1, HQ)],
        scratch_shapes=[pltpu.VMEM((rows, HQ * DH), F32)] * 3
        + [pltpu.VMEM((HQ, rows), F32), pltpu.SemaphoreType.DMA((4,))],
        compiler_params=pltpu.CompilerParams(vmem_limit_bytes=PACK_VMEM * 2**20),
        cost_estimate=pl.CostEstimate(flops=2**32, bytes_accessed=2**21, transcendentals=0),
        name="pack",
    )(rank, *[pltpu.with_memory_space_constraint(x, pltpu.HBM) for x in (order, query, grad_output, output, lse)])


def half_kernel(rank_ref, b_ref, out_ref):
    first = pl.multiple_of((rank_ref[0] % 2) * HALF, HALF)
    out_ref[:HALF] = b_ref[pl.ds(first, HALF)]
    out_ref[HALF:] = b_ref[pl.ds(first + 2 * HALF, HALF)]


def join_kernel(rank_ref, r_ref, r4_ref, later_ref, mine_ref, other_ref):
    first = pl.multiple_of((rank_ref[0] % 2) * HALF, HALF)
    mine_ref[...] = r_ref[: 2 * HALF]
    other_ref[...] = r_ref[2 * HALF :]
    mine_ref[pl.ds(first, HALF)] += r4_ref[:HALF]
    other_ref[pl.ds(first, HALF)] += r4_ref[HALF:]


def small(kernel, n, *args):
    shape = jax.ShapeDtypeStruct((2 * HALF, 2 * DH), F32)
    return pl.pallas_call(
        kernel,
        in_specs=[SM] + [VM if a.shape[1] == 2 * DH else pl.BlockSpec(memory_space=pl.ANY) for a in args[1:]],
        out_specs=[VM] * n,
        out_shape=[shape] * n,
        compiler_params=pltpu.CompilerParams(vmem_limit_bytes=4 * 2**20),
        name=kernel.__name__,
    )(*args)


def tie_kernel(x_ref, sign_ref, out_ref):
    pass


def names_of(jobs):
    names = []
    for gs, halves in jobs:
        for g in gs:
            names += [(g, None)] if g in ("self", "core") else [(g, half) for half in (0, *halves)]
    return list(dict.fromkeys(names))


def grads_kernel(steps, jobs, dq_from, dq_old, has_dkv, ties, *refs):
    refs = list(refs)
    take = lambda n: [refs.pop(0) for _ in range(n)]
    rank_ref, order_ref = take(2)
    groups = list(dict.fromkeys(g for gs, _ in jobs for g in gs))
    names = names_of(jobs)
    packs = dict(zip(names, take(len(names))))
    kv_refs = take(len(steps))
    dq_in = dict(zip(dq_from, take(len(dq_from))))
    dkv_in = dict(zip(has_dkv, take(len(has_dkv))))
    take(ties)
    dq_out = dict(zip(groups, take(len(groups))))
    dkv_out = take(len(steps))
    sign = refs.pop(0)
    sign[...] = jnp.zeros_like(sign)
    kc, vc = take(2)

    rank = rank_ref[0]
    z, xh, c = rank // 4, (rank // 2) % 2, rank % 2
    lane = lax.broadcasted_iota(jnp.int32, (HALF, DH), 1)
    at = 0
    for step, ref in zip(steps, kv_refs):
        zk = lax.rem(z + (2 * c - 1) * step + ZS, ZS)
        for i in range(ref.shape[0] // HALF):
            if step < ZS // 2:
                line, part = (c if i < 2 else 1 - c), i % 2
            else:
                line, part = (c if i < 1 else 1 - c), c
            pos = order_ref[(zk * 4 + xh * 2 + line) * 2 + part]
            hot = jnp.where((lane == pos) | (lane >= HALF), 1.0, 0.0).astype(BF16)
            s, to = slice(i * HALF, (i + 1) * HALF), slice(at, at + HALF)
            hi, lo = split(ref[s, :DH])
            kc[to, :] = jnp.concatenate([hi, lo, hi, hot], axis=1)
            hi, lo = split(ref[s, DH:])
            vc[to, :] = jnp.concatenate([hi, lo, hi, hot], axis=1)
            at += HALF

    lane = lax.broadcasted_iota(jnp.int32, (DH, DH), 1)
    first = True
    for gs, half in ((gs, half) for gs, halves in jobs for half in halves):
        qs, ds = [], []
        for h in range(CHUNK):
            head = half * CHUNK + h
            mine = (lane < HALF) | ((lane - HALF) // 3 == head)
            mine_do = (lane - HALF) // 3 == HQ + head
            for g in gs:
                if (g, None) in packs:
                    ref, q_at, do_at = packs[g, None], head * DH, (HQ + head) * DH
                    terms = ref[:, 2 * HQ * DH :]
                else:
                    ref, q_at, do_at = packs[g, half], h * DH, (CHUNK + h) * DH
                    terms = packs[g, 0][:, 2 * CHUNK * DH :]
                hi, lo = split(ref[:, q_at : q_at + DH])
                bias = jnp.where(mine, terms, 0.0).astype(BF16)
                qs.append(jnp.concatenate([hi, hi, lo, bias], axis=1))
                hi, lo = split(ref[:, do_at : do_at + DH])
                bias = jnp.where(mine_do, terms, 0.0).astype(BF16)
                ds.append(jnp.concatenate([hi, hi, lo, bias], axis=1))
        qc, dc = jnp.concatenate(qs, axis=0), jnp.concatenate(ds, axis=0)
        p = jnp.exp2(dot(kc[...], qc, NT))
        if 0 in steps and "self" in gs:
            top = p[:DH]
            a = lax.broadcasted_iota(jnp.int32, top.shape, 0)
            b = lax.broadcasted_iota(jnp.int32, top.shape, 1)
            rows = len(gs) * DH
            b = b - (b // rows) * rows - gs.index("self") * DH
            top = jnp.where((b >= 0) & (b < DH) & (a // HALF == b // HALF) & (a > b), 0.0, top)
            p = top if p.shape[0] == DH else jnp.concatenate([top, p[DH:]], axis=0)
        d = p * dot(vc[...], dc, NT)
        p_hi, p_lo = split(p)
        r = dot(p_hi, dc[:, DH : 3 * DH])
        dv = r[:, :DH] + r[:, DH:] + dot(p_lo, dc[:, :DH])
        d_hi, d_lo = split(d)
        r = dot(d_hi, qc[:, DH : 3 * DH])
        dk = (r[:, :DH] + r[:, DH:] + dot(d_lo, qc[:, :DH])) * (1.0 / LOG2E)
        at = 0
        for step, out in zip(steps, dkv_out):
            s = slice(at, at + out.shape[0])
            at += out.shape[0]
            if first:
                out[:, :DH] = dkv_in[step][:, :DH] + dk[s] if step in dkv_in else dk[s]
                out[:, DH:] = dkv_in[step][:, DH:] + dv[s] if step in dkv_in else dv[s]
            else:
                out[:, :DH] += dk[s]
                out[:, DH:] += dv[s]
        first = False
        r = dot(d_hi, kc[:, : 2 * DH], TN)
        dq = (r[:, :DH] + r[:, DH:] + dot(d_lo, kc[:, :DH], TN)) * (1.0 / math.sqrt(DH))
        for h in range(CHUNK):
            for j, g in enumerate(gs):
                s = slice((half * CHUNK + h) * DH, (half * CHUNK + h + 1) * DH)
                t = dq[(h * len(gs) + j) * DH : (h * len(gs) + j + 1) * DH]
                dq_out[g][:, s] = dq_in[g][:, s] + t if (g, half) in dq_old else t


class Totals:
    def __init__(self, rank, order, packs, blocks):
        self.rank, self.order, self.packs, self.blocks = rank, order, packs, blocks
        self.dq, self.held, self.dkv, self.last = {}, set(), {}, None

    def after(self, x):
        any_ = pl.BlockSpec(memory_space=pl.ANY)
        return pl.pallas_call(
            tie_kernel,
            in_specs=[any_, any_],
            out_specs=any_,
            out_shape=jax.ShapeDtypeStruct(x.shape, x.dtype),
            input_output_aliases={0: 0},
            compiler_params=pltpu.CompilerParams(vmem_limit_bytes=2**20),
            name="tie",
        )(x, self.last)

    def add(self, steps, *jobs, need=(), flops=2**10):
        groups = list(dict.fromkeys(g for gs, _ in jobs for g in gs))
        args = [self.packs[n] for n in names_of(jobs)] + [self.blocks[s] for s in steps]
        dq_from = [g for g in groups if g in self.dq]
        dq_old = frozenset(self.held)
        self.held.update((g, half) for gs, halves in jobs for g in gs for half in halves)
        has_dkv = [s for s in steps if s in self.dkv]
        aliases = {}
        for g in dq_from:
            aliases[2 + len(args)] = groups.index(g)
            args.append(self.dq[g])
        for s in has_dkv:
            aliases[2 + len(args)] = len(groups) + steps.index(s)
            args.append(self.dkv[s])
        ties = [*need] if self.last is None else [self.last, *need]
        args += ties
        rows = [self.blocks[s].shape[0] for s in steps]
        keys = sum(rows)
        outs = pl.pallas_call(
            functools.partial(grads_kernel, steps, jobs, dq_from, dq_old, has_dkv, len(ties)),
            in_specs=[SM, SM] + [VM] * (len(args) - len(ties)) + [pl.BlockSpec(memory_space=pl.ANY)] * len(ties),
            out_specs=[VM] * (len(groups) + len(steps) + 1),
            out_shape=[jax.ShapeDtypeStruct((DH, HQ * DH), F32)] * len(groups)
            + [jax.ShapeDtypeStruct((n, 2 * DH), F32) for n in rows]
            + [jax.ShapeDtypeStruct((8, DH), F32)],
            input_output_aliases=aliases,
            scratch_shapes=[pltpu.VMEM((keys, 4 * DH), BF16)] * 2,
            compiler_params=pltpu.CompilerParams(vmem_limit_bytes=(8 + keys // 40) * 2**20),
            cost_estimate=pl.CostEstimate(flops=flops, bytes_accessed=2**10, transcendentals=0),
            name="grads_" + "".join(map(str, steps)) + "_" + "_".join(gs[0] + "ab"[halves[0] : halves[-1] + 1] for gs, halves in jobs),
        )(self.rank, self.order, *args)
        self.dq.update(zip(groups, outs))
        self.dkv.update(zip(steps, outs[len(groups) : -1]))
        self.last = outs[-1]


def local(query, key, value, output, grad_output, lse, span_order):
    rank = lax.axis_index("ctx").astype(jnp.int32).reshape(1)
    c = rank[0] % 2
    kv = jnp.concatenate([key, value], axis=1)
    kv_c = send(kv, core)
    p, pa, pb = pack(rank, span_order, query, grad_output, output, lse)
    packs = {("self", None): p, ("x", 0): send(pa, chip), ("core", None): send(p, core)}
    blocks = {0: kv}
    total = Totals(rank, span_order, packs, blocks)
    after = total.after
    own, other = ("self", "core"), ("x", "v")
    both = (0, 1)
    blocks[1] = send(jnp.concatenate([kv, kv_c], axis=0), ring)
    total.add([0], (own, both))
    blocks[1] = after(blocks[1])
    blocks[2] = send(blocks[1], ring)
    total.add([1], (own, both))
    packs["x", 0] = after(packs["x", 0])
    packs["v", 0] = send(packs["x", 0], core)
    packs["x", 1] = send(after(pb), chip)
    blocks[2] = after(blocks[2])
    blocks[3] = send(blocks[2], ring)
    total.add([2], (own, both), flops=2**37)
    total.add([0, 1, 2], (other, (0,)))
    blocks[3] = after(blocks[3])
    blocks[4] = send(small(half_kernel, 1, rank, blocks[3])[0], ring)
    total.add([3], (own, both))
    packs["x", 1] = after(packs["x", 1])
    packs["v", 1] = send(packs["x", 1], core)
    total.add([3], (other, (0,)), need=[blocks[4]], flops=2**37)
    total.add([3], (other, (1,)))
    r = send(total.dkv[3], ring, back=True)
    total.add([4], (other, both), (own, both), flops=2**37)
    total.add([0, 1, 2], (other, (1,)), need=[r])
    r = send(total.dkv[2] + r, ring, back=True)
    dq_x = total.dq["x"] + send(total.dq["v"], core)
    dq_x = send(dq_x, chip, back=True)
    r4 = send(total.dkv[4], across)
    r = send(total.dkv[1] + r, ring, back=True)
    r, r_c = small(join_kernel, 2, rank, r, r4, dq_x)
    dkv = total.dkv[0] + r + send(r_c, core)
    dq = total.dq["self"] + send(total.dq["core"], core) + dq_x
    return dq, dkv[:, :DH], dkv[:, DH:]


def solution(mesh):
    in_specs = (
        P("ctx", "heads"),
        P("ctx", "heads"),
        P("ctx", "heads"),
        P("ctx", "heads"),
        P("ctx", "heads"),
        P("heads", "ctx"),
        P("heads"),
    )
    out_specs = (P("ctx", "heads"), P("ctx", "heads"), P("ctx", "heads"))
    return jax.shard_map(local, mesh=mesh, in_specs=in_specs, out_specs=out_specs, check_vma=False)
```
